128 devices in a mesh: grp: 4 (over x), ctx: 16 (over y, z_lo, core), tp: 2 (over z_hi).
Axes of the slice: x: 4, y: 4, z: 4 (z_hi: 2, z_lo: 2; z = z_hi * 2 + z_lo), core: 2. Of those that a mesh axis runs over, the one named last changes fastest.
Arguments:
- trunk_out: bfloat16 [2048, 4096], P('ctx', ('grp', 'tp')), may hold values from -6 to 6
- norm_gain: bfloat16 [4, 4096], P('grp', 'ctx'), may hold values from 0.099609375 to 1.8984375
- w_query: bfloat16 [4, 4096, 4096], P('grp', 'ctx', 'tp'), may hold values from -2.34375 to 2.34375
- w_key: bfloat16 [4, 4096, 512], P('grp', 'ctx', 'tp'), may hold values from -0.078125 to 0.078125
- value_weight: bfloat16 [4, 4096, 512], P('grp', 'ctx', 'tp'), may hold values from -0.09375 to 0.09375
- context_gradient: bfloat16 [4, 2048, 4096], P('grp', 'ctx', 'tp'), may hold values from -6 to 6
Outputs:
- trunk_grad: float32 [2048, 4096], P('ctx', ('grp', 'tp'))
The draws below stay inside these ranges and needn't reach their ends.
All inputs are finite; a program needn't handle non-finite values.
Results may differ from the reference program's by a relative error of at most 0.008.
Values may be sent and summed in bfloat16 or wider, within the bound.
A program may use at most 128 MiB of HBM per device.

```python
import jax
import jax.numpy as jnp
from jax import lax

TRUNK_WIDTH = 4096
QUERY_HEAD_COUNT = 32
KEY_VALUE_HEADS = 4
HEAD_SIZE = 128
S = 2048
PREDICT_HEADS = 4


def key_base(key):
    return jnp.clip(jax.random.normal(key, (PREDICT_HEADS, TRUNK_WIDTH, KEY_VALUE_HEADS * HEAD_SIZE), jnp.float32), -5.0, 5.0)


def draw_w_key(key, part):
    base_offset = key_base(key)
    return (base_offset * TRUNK_WIDTH ** (-0.5)).astype(jnp.bfloat16)


def draw_w_query(key, part):
    key = jax.random.fold_in(key, 23)
    per_group_count = QUERY_HEAD_COUNT // KEY_VALUE_HEADS
    own_slice = jnp.clip(jax.random.normal(key, (PREDICT_HEADS, TRUNK_WIDTH, KEY_VALUE_HEADS, per_group_count, HEAD_SIZE), jnp.float32), -5.0, 5.0) * TRUNK_WIDTH ** (-0.5)
    return own_slice.reshape(PREDICT_HEADS, TRUNK_WIDTH, QUERY_HEAD_COUNT * HEAD_SIZE).astype(jnp.bfloat16)


def steps_of(stream_key, extent, split, low, high):
    loudness = 1.0
    for dim, blocks in split:
        steps = jax.random.uniform(jax.random.fold_in(jax.random.fold_in(stream_key, 6), dim), (blocks,), jnp.float32, low / len(split), high / len(split))
        loudness = loudness * jnp.repeat(jnp.exp(steps), extent[dim] // blocks).reshape((-1,) + (1,) * (len(extent) - 1 - dim))
    return loudness


def scatter_about(rng, dims, deviation, most, shards=(), held_as=jnp.bfloat16):
    values = jax.random.normal(rng, dims, jnp.float32) * deviation
    if len(shards) > 0:
        values = steps_of(rng, dims, shards, -0.22, 0.18) * values
    return jnp.clip(values, min=-most, max=most).astype(held_as)


def setup_inputs(seed: int = 0) -> dict:
    splits = jax.random.split(jax.random.key(seed), 7)
    trunk_out = scatter_about(splits[0], (S, TRUNK_WIDTH), 1.0, 6.0, ((0, 16), (1, 8)))
    norm_gain = jnp.clip(1.0 + 0.18 * jax.random.normal(splits[1], (PREDICT_HEADS, TRUNK_WIDTH), jnp.float32), 0.099609375, 1.8984375).astype(jnp.bfloat16)
    w_query = draw_w_query(jax.random.fold_in(splits[6], 71), 0)
    w_key = draw_w_key(jax.random.fold_in(splits[6], 71), 0)
    value_weight = scatter_about(splits[4], (PREDICT_HEADS, TRUNK_WIDTH, KEY_VALUE_HEADS * HEAD_SIZE), TRUNK_WIDTH ** -0.5, 0.09375, ((0, 4), (1, 16), (2, 2)))
    context_gradient = scatter_about(splits[5], (PREDICT_HEADS, S, QUERY_HEAD_COUNT * HEAD_SIZE), 1.0, 6.0, ((0, 4), (1, 16), (2, 2)))
    return dict(trunk_out=trunk_out, norm_gain=norm_gain, w_query=w_query, w_key=w_key, value_weight=value_weight, context_gradient=context_gradient)


EPSILON = 1e-05
MASKED_SCORE = -1e+30
PRECISE = lax.Precision.HIGHEST

def kv_head_backward(operands):
    query_rows, key_row_block, value_row_block, grad_rows = operands
    positions = jnp.arange(key_row_block.shape[0])
    allowed = positions[None, :] <= positions[:, None]
    query_f32 = query_rows.astype(jnp.float32)
    key_f32 = key_row_block.astype(jnp.float32)
    value_f32 = value_row_block.astype(jnp.float32)
    grad_f32 = grad_rows.astype(jnp.float32)
    score_scale = HEAD_SIZE ** (-0.5)
    scores = jnp.einsum('igd,jd->gij', query_f32, key_f32, precision=PRECISE) * score_scale
    scores = jnp.where(allowed[None], scores, MASKED_SCORE)
    top_score = lax.optimization_barrier(jnp.max(scores, axis=-1, keepdims=True))
    exp_terms = jnp.exp(scores - top_score)
    probs_f32 = exp_terms / lax.optimization_barrier(jnp.sum(exp_terms, axis=-1, keepdims=True))
    context = jnp.einsum('gij,jd->igd', probs_f32, value_f32, precision=PRECISE)
    row_delta = lax.optimization_barrier(jnp.sum(grad_f32 * context, axis=-1))
    probs_low = lax.optimization_barrier(probs_f32.astype(jnp.bfloat16)).astype(jnp.float32)
    value_gradient = jnp.einsum('gij,igd->jd', probs_low, grad_f32, precision=PRECISE)
    prob_grad = jnp.einsum('igd,jd->gij', grad_f32, value_f32, precision=PRECISE)
    score_grad = probs_f32 * (prob_grad - jnp.transpose(row_delta)[:, :, None]) * score_scale
    score_low = lax.optimization_barrier(score_grad.astype(jnp.bfloat16)).astype(jnp.float32)
    query_grad = jnp.einsum('gij,jd->igd', score_low, key_f32, precision=PRECISE).astype(jnp.bfloat16)
    key_gradient = jnp.einsum('gij,igd->jd', score_low, query_f32, precision=PRECISE)
    return (query_grad, key_gradient, value_gradient)

def reference(trunk_out, norm_gain, w_query, w_key, value_weight, context_gradient):
    sequence_rows = trunk_out.shape[0]
    per_group_count = QUERY_HEAD_COUNT // KEY_VALUE_HEADS
    trunk_f32 = trunk_out.astype(jnp.float32)
    inverse = lax.rsqrt(lax.optimization_barrier(jnp.mean(trunk_f32 * trunk_f32, axis=1, keepdims=True)) + EPSILON)
    scaled = trunk_f32 * inverse
    total_grad = jnp.zeros(trunk_f32.shape, jnp.float32)
    for head_number in range(PREDICT_HEADS):
        gain_row = norm_gain[head_number].astype(jnp.float32)
        normed = (scaled * gain_row[None, :]).astype(jnp.bfloat16)
        query_rows = jnp.dot(normed, w_query[head_number], preferred_element_type=jnp.float32).astype(jnp.bfloat16)
        key_row_block = jnp.dot(normed, w_key[head_number], preferred_element_type=jnp.float32).astype(jnp.bfloat16)
        value_row_block = jnp.dot(normed, value_weight[head_number], preferred_element_type=jnp.float32).astype(jnp.bfloat16)
        stacked_heads = (jnp.transpose(query_rows.reshape(sequence_rows, KEY_VALUE_HEADS, per_group_count, HEAD_SIZE), (1, 0, 2, 3)), jnp.transpose(key_row_block.reshape(sequence_rows, KEY_VALUE_HEADS, HEAD_SIZE), (1, 0, 2)), jnp.transpose(value_row_block.reshape(sequence_rows, KEY_VALUE_HEADS, HEAD_SIZE), (1, 0, 2)), jnp.transpose(context_gradient[head_number].reshape(sequence_rows, KEY_VALUE_HEADS, per_group_count, HEAD_SIZE), (1, 0, 2, 3)))
        query_grad, key_gradient, value_gradient = lax.map(kv_head_backward, stacked_heads)
        query_grad = jnp.transpose(query_grad, (1, 0, 2, 3)).reshape(sequence_rows, QUERY_HEAD_COUNT * HEAD_SIZE)
        key_narrow = jnp.transpose(key_gradient, (1, 0, 2)).reshape(sequence_rows, KEY_VALUE_HEADS * HEAD_SIZE).astype(jnp.bfloat16)
        value_narrow = jnp.transpose(value_gradient, (1, 0, 2)).reshape(sequence_rows, KEY_VALUE_HEADS * HEAD_SIZE).astype(jnp.bfloat16)
        normed_grad = jnp.dot(query_grad, w_query[head_number].T, preferred_element_type=jnp.float32)
        normed_grad = normed_grad + jnp.dot(key_narrow, w_key[head_number].T, preferred_element_type=jnp.float32)
        normed_grad = normed_grad + jnp.dot(value_narrow, value_weight[head_number].T, preferred_element_type=jnp.float32)
        gained = normed_grad * gain_row[None, :]
        head_grad = inverse * gained - trunk_f32 * inverse ** 3 * lax.optimization_barrier(jnp.mean(trunk_f32 * gained, axis=1, keepdims=True))
        total_grad = total_grad + head_grad
    return total_grad
```

```python
import jax
import jax.numpy as jnp
from jax import lax
from jax.experimental import pallas as pl
from jax.experimental.pallas import tpu as pltpu
from jax.sharding import PartitionSpec as P

HEAD_SIZE = 128
EPSILON = 1e-05
MASKED_SCORE = -1e30
LOG2E = 1.4426950408889634
MESH = pl.DeviceIdType.MESH
ANY = pl.BlockSpec(memory_space=pl.ANY)
BF16 = jnp.bfloat16
F32 = jnp.float32
ROWS = 512
OUT_COLS = 4096
Q_COLS = 512
W_COLS = 640


class Place:
    def __init__(self):
        self.x = lax.axis_index("grp")
        ctx = lax.axis_index("ctx")
        self.ctx = ctx
        self.zh = lax.axis_index("tp")
        self.y = lax.div(ctx, 4)
        self.j = lax.rem(ctx, 4)
        self.zl = lax.div(self.j, 2)
        self.c = lax.rem(ctx, 2)
        self.z = self.zh * 2 + self.zl
        self.known = {}
        for dc in range(2):
            self.keep(dc=dc)
            self.keep(dzl=1, dc=dc)
        for d in range(1, 4):
            self.keep(dx=d)
            self.keep(dy=d)
            self.keep(dz=d)

    def keep(self, **deltas):
        deltas = {key: value for key, value in deltas.items() if value}
        self.known[tuple(sorted(deltas.items()))] = self.work_out(**deltas)

    def at(self, **deltas):
        deltas = {key: value for key, value in deltas.items() if not isinstance(value, int) or value}
        key = tuple(sorted(deltas.items()))
        return self.known[key] if key in self.known else self.work_out(**deltas)

    def work_out(self, dx=0, dy=0, dzl=0, dc=0, dz=0):
        def moved(value, step, size):
            return value if isinstance(step, int) and step == 0 else lax.rem(value + step, size)

        x, y, c = moved(self.x, dx, 4), moved(self.y, dy, 4), moved(self.c, dc, 2)
        zl, zh = moved(self.zl, dzl, 2), self.zh
        if dz:
            z = moved(self.z, dz, 4)
            zl, zh = lax.rem(z, 2), lax.div(z, 2)
        return {"grp": x, "ctx": y * 4 + zl * 2 + c, "tp": zh}


def greet(place, partners):
    barrier = pltpu.get_barrier_semaphore()
    for partner in partners:
        pl.semaphore_signal(barrier, inc=1, device_id=place.at(**partner), device_id_type=MESH)
    pl.semaphore_wait(barrier, len(partners))


def remote(src, dst, send_sem, recv_sem, device):
    return pltpu.make_async_remote_copy(
        src_ref=src, dst_ref=dst, send_sem=send_sem, recv_sem=recv_sem, device_id=device, device_id_type=MESH
    )


J_OTHERS = [dict(dc=1), dict(dzl=1), dict(dzl=1, dc=1)]
PARTNERS = J_OTHERS + [{axis: d} for axis in ("dx", "dy", "dz") for d in (1, 2, 3)]
GATHER_ROWS = ((0, 96), (96, 32))
SUM_ROWS = ((0, 48), (48, 80))


def mm(a, b, contract):
    return lax.dot_general(a, b, ((contract[:1], contract[1:]), ((), ())), preferred_element_type=F32)


def go(src, dst, send_sem, recv_sem, device):
    remote(src, dst, send_sem, recv_sem, device).start()


def arrived(ref, sem):
    pltpu.make_async_copy(ref, ref, sem).wait()


def lanes(index, width=128):
    return pl.ds(pl.multiple_of(index * width, width), width)


def backward_kernel(
    trunk, gain, wq, wk, wv, grads,
    out,
    wq_in, wk_in, wv_in, g_in, kv_cut, q_cut, g_cut,
    x_all, w_kv, w_q, d_all, inv_ref, gains, gain_rows, normed, q_all, g_all, kv, kt, q_turned, g_turned, g_pair, tiles, tops, dq_ref, dk_ref, dv_ref,
    dkv, core_in, back,
    dot_acc, sums, dots,
    relay_in_0, relay_out_0, near_in_0, last_sum_0, last_out_0, last_in_0,
    relay_in_1, relay_out_1, near_in_1, last_sum_1, last_out_1, last_in_1,
    w_send, w_recv, w_set, x_send, x_recv, x_core, gain_send, gain_recv, gain_set, g_send, g_recv,
    kv_send, kv_recv, core_send, core_recv, back_send, back_recv, local,
    swap_send, swap_recv, near_send, near_recv, last_send, last_recv, dot_send, dot_recv,
):
    relay_in, relay_out, near_in = (relay_in_0, relay_in_1), (relay_out_0, relay_out_1), (near_in_0, near_in_1)
    last_sum, last_out, last_in = (last_sum_0, last_sum_1), (last_out_0, last_out_1), (last_in_0, last_in_1)
    p = Place()
    pairs = ((wk.at[0], wk_in), (wv.at[0], wv_in), (wq.at[0], wq_in), (grads.at[0], g_in))
    loads = [pltpu.make_async_copy(src, dst, local.at[i]) for i, (src, dst) in enumerate(pairs)]
    for load in loads:
        load.start()
    greet(p, PARTNERS)

    def j_of(dzl=0, dc=0):
        return lax.rem(p.zl + dzl, 2) * 2 + lax.rem(p.c + dc, 2)

    below, above, across = [lax.rem(p.y + d, 4) for d in (3, 1, 2)]
    j_others = [(j_of(**other), p.at(**other)) for other in J_OTHERS]

    def w_of(piece):
        return w_q.at[piece - 1] if piece else w_kv

    def w_cut(piece):
        return q_cut.at[piece - 1] if piece else kv_cut

    def w_first(piece):
        cut, ref = w_cut(piece), w_of(piece)
        for j in range(4):
            if piece:
                column = j * Q_COLS + (piece - 1) * 256
                cut[j] = wq_in[:, column : column + 256]
            else:
                cut[j] = (wv_in if j % 2 else wk_in)[:, 128 * (j // 2) : 128 * (j // 2) + 128]
        for i, (j, device) in enumerate(j_others):
            go(cut.at[j], ref.at[p.ctx], w_send.at[piece, i], w_recv.at[piece, p.j], device)
        ref[p.ctx] = cut[p.j]

    def w_part(piece, y, part):
        return w_of(piece).at[pl.ds(4 * y + 2 * part, 2)]

    def w_go(piece, y, part, slot, device):
        ref = w_part(piece, y, part)
        go(ref, ref, w_send.at[piece, slot], w_set.at[piece, y, part], device)

    def w_wait(piece, y, part):
        arrived(w_part(piece, y, part), w_set.at[piece, y, part])

    def w_near(piece):
        j, _ = j_others[0]
        arrived(w_of(piece).at[p.y * 4 + j], w_recv.at[piece, j])
        w_go(piece, p.y, p.zl, 3, p.at(dy=1))
        w_go(piece, p.y, p.zl, 4, p.at(dy=3))

    def w_far(piece):
        for j, _ in j_others[1:]:
            arrived(w_of(piece).at[p.y * 4 + j], w_recv.at[piece, j])
        w_go(piece, p.y, 1 - p.zl, 5, p.at(dy=1))
        w_go(piece, p.y, 1 - p.zl, 6, p.at(dy=3))

    def w_relay(piece):
        w_wait(piece, below, 0)
        w_go(piece, below, 0, 7, p.at(dy=1))
        w_wait(piece, above, 1)
        w_go(piece, above, 1, 8, p.at(dy=3))

    def w_rest(piece):
        w_wait(piece, below, 1)
        w_wait(piece, above, 0)
        w_wait(piece, across, 0)
        w_wait(piece, across, 1)

    def x_a(half, d):
        return lax.rem((p.x if half else p.z) + d, 4)

    def x_b(half, d):
        return lax.rem((p.z if half else p.x) + d, 4)

    def a_device(half, da):
        return p.at(dx=da) if half else p.at(dz=da)

    def b_device(half, db):
        return p.at(dz=db) if half else p.at(dx=db)

    def x_piece(half, x, z):
        return x_all.at[lax.rem(z, 2), p.c, x, lax.div(z, 2), pl.ds(*GATHER_ROWS[half])]

    def x_full(half, b, c):
        if half:
            return x_all.at[lax.rem(b, 2), c, :, lax.div(b, 2), pl.ds(*GATHER_ROWS[1])]
        return x_all.at[:, c, b, :, pl.ds(*GATHER_ROWS[0])]

    def x_at(half, da, db):
        a, b = x_a(half, da), x_b(half, db)
        return (x_piece(1, a, b) if half else x_piece(0, b, a)), x_recv.at[half, a, b]

    def x_go(half, da, db, slot, device, src=None):
        dst, sem = x_at(half, da, db)
        go(dst if src is None else src, dst, x_send.at[half, slot], sem, device)

    def x_first(half):
        own = trunk.at[pl.ds(*GATHER_ROWS[half])]
        for i, d in enumerate((2, 1, 3)):
            x_go(half, 0, 0, i, a_device(half, d), own)
        x_go(half, 0, 0, 3, b_device(half, 1), own)
        x_go(half, 0, 0, 4, b_device(half, 3), own)

    def x_second(half):
        for i, d in enumerate((1, 3, 2)):
            arrived(*x_at(half, d, 0))
            x_go(half, d, 0, 5 + 2 * i, b_device(half, 1))
            x_go(half, d, 0, 6 + 2 * i, b_device(half, 3))

    def x_relay(half):
        for i in range(2):
            arrived(*x_at(half, i, 3))
            x_go(half, i, 3, 11 + 2 * i, b_device(half, 1))
            arrived(*x_at(half, 2 + i, 1))
            x_go(half, 2 + i, 1, 12 + 2 * i, b_device(half, 3))

    def x_to_core(half, d):
        b = x_b(half, d)
        ref = x_full(half, b, p.c)
        go(ref, ref, x_send.at[half, 15 + d], x_core.at[half, b], p.at(dc=1))

    halves = (0, 1)
    for half in halves:
        x_first(half)
    loads[0].wait()
    loads[1].wait()
    w_first(0)
    own_x = x_all.at[p.zl, p.c, p.x, p.zh]
    pltpu.make_async_copy(trunk, own_x, local.at[5]).start()
    gains[p.ctx] = jnp.broadcast_to(gain[...], (16, 256))
    for i, (j, device) in enumerate(j_others):
        go(gains.at[p.ctx], gains.at[p.ctx], gain_send.at[i], gain_recv.at[p.j], device)
    w_near(0)
    for half in halves:
        x_second(half)
    w_far(0)
    loads[2].wait()
    w_first(1)
    pltpu.make_async_copy(own_x, own_x, local.at[5]).wait()
    for half in halves:
        x_to_core(half, 0)
    for half in halves:
        x_relay(half)
    w_near(1)
    for j, _ in j_others:
        arrived(gains.at[p.y * 4 + j], gain_recv.at[j])
    gain_y = gains.at[pl.ds(4 * p.y, 4)]
    for dy in (1, 2, 3):
        go(gain_y, gain_y, gain_send.at[2 + dy], gain_set.at[p.y], p.at(dy=dy))
    w_far(1)
    w_relay(0)
    for half in halves:
        for i in range(2):
            arrived(*x_at(half, 2 + i, 3))
            arrived(*x_at(half, i, 1))
        x_to_core(half, 3)
        x_to_core(half, 1)
    w_first(2)
    for half in halves:
        for i in range(4):
            arrived(*x_at(half, i, 2))
        x_to_core(half, 2)
    loads[3].wait()
    for j in range(4):
        g_cut[j] = g_in[:, Q_COLS * j : Q_COLS * j + Q_COLS]
    for i, (j, device) in enumerate(j_others):
        go(g_cut.at[j], g_all.at[p.j], g_send.at[i], g_recv.at[p.j], device)
    g_all[p.j] = g_cut[p.j]
    w_near(2)
    for d in (1, 2, 3):
        y = lax.rem(p.y + d, 4)
        arrived(gains.at[pl.ds(4 * y, 4)], gain_set.at[y])
    for block in range(8):
        row = jnp.concatenate([gains[2 * block][:1], gains[2 * block + 1][:1]], axis=1)
        gain_rows[block] = jnp.broadcast_to(row.astype(F32), (8, 512))
    w_relay(1)
    for half in halves:
        for b in range(4):
            arrived(x_full(half, b, 1 - p.c), x_core.at[half, b])

    @pl.loop(0, 16)
    def _(step):
        group = lax.div(step, 4)
        rows = pl.ds(pl.multiple_of(lax.rem(step, 4) * 32, 32), 32)
        zl, c = lax.div(group, 2), lax.rem(group, 2)
        total = jnp.zeros((32, 128), F32)
        for block in range(8):
            part = x_all[zl, c, block // 2, block % 2, rows].astype(F32)
            part = part * part
            total = total + ((part[:, :128] + part[:, 128:256]) + (part[:, 256:384] + part[:, 384:]))
        inverse = lax.rsqrt(jnp.sum(total, axis=1, keepdims=True) * (1.0 / OUT_COLS) + EPSILON)
        inverse = jnp.broadcast_to(inverse, (32, 128))
        inv_ref[zl, c, rows] = inverse
        wide = jnp.concatenate([inverse] * 4, axis=1)
        for block in range(8):
            scaled = x_all[zl, c, block // 2, block % 2, rows].astype(F32) * wide
            scaled = scaled.reshape(4, 8, 512) * gain_rows[block][None]
            row = pl.ds(pl.multiple_of(step * 32, 32), 32)
            normed[block, row] = scaled.reshape(32, 512).astype(BF16)

    def project(piece):
        ref, width = w_of(piece), 256 if piece else 128

        def step(block, acc):
            right = ref[pl.ds(8 * block, 8)].reshape(2048, width)
            left = jnp.concatenate([normed[4 * block + i] for i in range(4)], axis=1)
            return acc + jnp.dot(left, right, preferred_element_type=F32)

        return lax.fori_loop(0, 2, step, jnp.zeros((ROWS, width), F32)).astype(BF16)

    def project_heads(piece):
        q = project(piece)
        for i in range(2):
            q_all[2 * piece - 2 + i] = q[:, 128 * i : 128 * i + 128]
            q_turned[2 * piece - 2 + i] = jnp.transpose(q[:, 128 * i : 128 * i + 128])

    w_rest(0)
    kv[p.c, p.y] = project(0)
    own_kv = kv.at[p.c, p.y]
    for dy in (1, 2, 3):
        @pl.when(p.y + dy < 4)
        def _():
            go(own_kv, own_kv, kv_send.at[dy - 1], kv_recv.at[p.c, p.y], p.at(dy=dy))

    go(own_kv, own_kv, kv_send.at[3], kv_recv.at[p.c, p.y], p.at(dc=1))
    w_far(2)
    w_rest(1)
    project_heads(1)
    for dy in (1, 3, 2):
        @pl.when(p.y >= dy)
        def _():
            ref = kv.at[p.c, p.y - dy]
            arrived(ref, kv_recv.at[p.c, p.y - dy])
            go(ref, ref, kv_send.at[3 + dy], kv_recv.at[p.c, p.y - dy], p.at(dc=1))

    for j, _ in j_others:
        arrived(g_all.at[j], g_recv.at[j])
    w_relay(2)
    for dy in (0, 1, 3, 2):
        @pl.when(p.y >= dy)
        def _():
            arrived(kv.at[1 - p.c, p.y - dy], kv_recv.at[1 - p.c, p.y - dy])

    scale = HEAD_SIZE ** -0.5
    factor = scale * LOG2E
    dk_ref[...] = jnp.zeros_like(dk_ref)
    dv_ref[...] = jnp.zeros_like(dv_ref)

    @pl.loop(0, p.y + 1)
    def _(block):
        kt[block] = jnp.transpose(kv[0, block])

    def fold(value, combine):
        parts = [value[8 * i : 8 * i + 8] for i in range(4)]
        return combine(combine(parts[0], parts[1]), combine(parts[2], parts[3]))

    def over(row, count):
        return jnp.broadcast_to(row, (count, ROWS))

    def statistics(head, block, s, t, state, diagonal):
        top, total, delta = state
        tiles[head, 1, block] = t
        parts = [s[32 * i : 32 * i + 32] for i in range(16)]
        if diagonal:
            key = lax.broadcasted_iota(jnp.int32, (32, ROWS), 0)
            row = lax.broadcasted_iota(jnp.int32, (32, ROWS), 1)
            parts = [jnp.where(key <= row - 32 * i, part, MASKED_SCORE) for i, part in enumerate(parts)]
        most = fold(parts[0], jnp.maximum)
        for part in parts[1:]:
            most = jnp.maximum(most, fold(part, jnp.maximum))
        now = jnp.maximum(top, jnp.max(most, axis=0, keepdims=True))
        tops[head, block] = over(now, 8)
        wide = over(now, 32)
        sums = jnp.zeros((8, ROWS), F32)
        deltas = jnp.zeros((8, ROWS), F32)
        for i, part in enumerate(parts):
            e = jnp.exp2((part - wide) * factor)
            tiles[head, 0, block, 32 * i : 32 * i + 32] = e
            sums = sums + fold(e, jnp.add)
            deltas = deltas + fold(e * t[32 * i : 32 * i + 32], jnp.add)
        shrink = jnp.exp2((top - now) * factor)
        total = total * shrink + jnp.sum(sums, axis=0, keepdims=True)
        delta = delta * shrink + jnp.sum(deltas, axis=0, keepdims=True)
        return now, total, delta

    def scores(pair, block, states, diagonal):
        products = []
        for head in range(2):
            s = mm(kv[0, block], q_turned[2 * pair + head], (1, 0))
            products.append((s, mm(kv[1, block], g_turned[head], (1, 0))))
        return tuple(statistics(i, block, *products[i], states[i], diagonal) for i in range(2))

    def lows(head, block, stats):
        top, inverse, delta = stats
        weight = over(jnp.exp2((tops[head, block][:1] - top) * factor) * inverse, 32)
        wide = over(delta, 32)
        probs_low, ds_low = [], []
        for i in range(16):
            chunk = pl.ds(32 * i, 32)
            probs = tiles[head, 0, block, chunk] * weight
            probs_low.append(probs.astype(BF16))
            ds_low.append((probs * (tiles[head, 1, block, chunk] - wide)).astype(BF16))
        return jnp.concatenate(probs_low, axis=0), jnp.concatenate(ds_low, axis=0)

    def pair_grads(pair, block, stats):
        both = [lows(head, block, stats[head]) for head in range(2)]
        for head in range(2):
            dq_ref[head] += mm(kt[block], both[head][1], (1, 0))
        probs = jnp.concatenate([both[0][0], both[1][0]], axis=1)
        ds = jnp.concatenate([both[0][1], both[1][1]], axis=1)
        dv_ref[block] += mm(probs, g_pair[...], (1, 0))
        dk_ref[block] += mm(ds, q_all[pl.ds(2 * pair, 2)].reshape(2 * ROWS, HEAD_SIZE), (1, 0))

    def core_go(block):
        return remote(dkv.at[1 - p.c, block], core_in.at[block], core_send.at[block], core_recv.at[block], p.at(dc=1))

    def back_go(block):
        device = {"grp": p.x, "ctx": block * 4 + p.j, "tp": p.zh}
        return remote(dkv.at[p.c, block], back.at[p.y], back_send.at[block], back_recv.at[p.y], device)

    def to_core(block):
        dkv[0, block] = (dk_ref[block] * scale).astype(BF16)
        dkv[1, block] = dv_ref[block].astype(BF16)
        core_go(block).start()

    def to_rows(block):
        core_go(block).wait_recv()
        dkv[p.c, block] = (dkv[p.c, block].astype(F32) + core_in[block].astype(F32)).astype(BF16)
        back_go(block).start()

    @pl.loop(0, 2)
    def _(pair):
        @pl.when(pair == 1)
        def _():
            w_rest(2)
            project_heads(2)

        for head in range(2):
            g = g_all[:, :, lanes(2 * pair + head)].reshape(ROWS, HEAD_SIZE)
            g_pair[ROWS * head : ROWS * head + ROWS] = g
            g_turned[head] = jnp.transpose(g)
        dq_ref[...] = jnp.zeros_like(dq_ref)
        start = (jnp.full((1, ROWS), MASKED_SCORE, F32), jnp.zeros((1, ROWS), F32), jnp.zeros((1, ROWS), F32))
        states = lax.fori_loop(0, p.y, lambda block, now: scores(pair, block, now, False), (start, start))
        states = scores(pair, p.y, states, True)
        stats = []
        for top, total, delta in states:
            inverse = 1.0 / total
            stats.append((top, inverse, delta * inverse))

        @pl.loop(0, p.y + 1)
        def _(block):
            pair_grads(pair, block, stats)

            @pl.when(pair == 1)
            def _():
                to_core(block)

                @pl.when(block > 0)
                def _():
                    to_rows(block - 1)

        for head in range(2):
            dq = jnp.transpose(dq_ref[head] * scale).astype(BF16)
            d_all[:, :, :, lanes(2 * pair + head + 1)] = dq.reshape(2, 2, 128, HEAD_SIZE)

    core_go(p.y).wait_recv()
    dk_ref[0] = dkv[p.c, p.y].astype(F32) + core_in[p.y].astype(F32)
    for dy in (1, 2, 3):
        @pl.when(p.y + dy < 4)
        def _():
            arrived(back.at[p.y + dy], back_recv.at[p.y + dy])
            dk_ref[0] += back[p.y + dy].astype(F32)
    d_all[:, :, :, :128] = dk_ref[0].astype(BF16).reshape(2, 2, 128, HEAD_SIZE)

    dot_acc[...] = jnp.zeros_like(dot_acc)

    def tile_rows(zl, c, i):
        return pl.ds(pl.multiple_of((zl * 2 + c) * 128 + 32 * i, 32), 32)

    def out_block(x, zh):
        block = x * 2 + zh
        left = d_all[...].reshape(ROWS, W_COLS)
        right = [w_of(piece)[pl.ds(2 * block, 2)].reshape(512, 256 if piece else 128) for piece in range(3)]
        part = mm(left, jnp.concatenate(right, axis=1), (1, 1))
        gain_row = gain_rows[block][None]
        for zl in range(2):
            for c in range(2):
                for i in range(4):
                    rows = slice(32 * i, 32 * i + 32)
                    first = (zl * 2 + c) * 128 + 32 * i
                    piece = (part[first : first + 32].reshape(4, 8, 512) * gain_row).reshape(32, 512)
                    tiles[zh, 0, x, first : first + 32] = piece
                    piece = piece * x_all[zl, c, x, zh, rows].astype(F32)
                    piece = (piece[:, :128] + piece[:, 128:256]) + (piece[:, 256:384] + piece[:, 384:])
                    dot_acc[zl, c, rows] += piece
        for zl in range(2):
            for i in range(4):
                rows = slice(32 * i, 32 * i + 32)
                normed[2 * x + zh, 128 * zl + 32 * i : 128 * zl + 32 * i + 32] = tiles[zh, 0, x, tile_rows(zl, 1 - p.c, i)].astype(BF16)

    def swap_out(x, zh):
        return normed.at[2 * x + zh, pl.ds(0, 256)]

    def swap_in(x, zh):
        return normed.at[2 * x + zh, pl.ds(256, 256)]

    def swap(x, zh):
        return remote(swap_out(x, zh), swap_in(x, zh), swap_send.at[x, zh], swap_recv.at[x, zh], p.at(dc=1))

    def out_blocks(x):
        @pl.loop(0, 2)
        def _(zh):
            out_block(x, zh)
            swap(x, zh).start()

    def add_blocks(x):
        @pl.loop(0, 2)
        def _(zh):
            swap(x, zh).wait_recv()
            for zl in range(2):
                for i in range(4):
                    rows = pl.ds(32 * i, 32)
                    total = tiles[zh, 0, x, tile_rows(zl, p.c, i)] + normed[2 * x + zh, 256 + 128 * zl + 32 * i : 288 + 128 * zl + 32 * i].astype(F32)
                    sums[x, zh, zl, rows] = total.astype(BF16)

    def mine(half, da, part):
        a = x_a(half, da)
        if half:
            return sums.at[a, part, :, pl.ds(*SUM_ROWS[1])]
        return sums.at[pl.ds(2 * part, 2), lax.div(a, 2), lax.rem(a, 2), pl.ds(*SUM_ROWS[0])]

    def near_go(half, way, kind):
        step = 3 if way else 1
        if kind == 0:
            src, dst = mine(half, 2, way), relay_in[half].at[way]
        elif kind == 1:
            src, dst = mine(half, step, 1 - way), near_in[half].at[way, 1 - way]
        else:
            src, dst = relay_out[half].at[way], near_in[half].at[way, way]
        return remote(src, dst, near_send.at[half, way, kind], near_recv.at[half, way, kind], a_device(half, step))

    def relay(half, way):
        near_go(half, way, 0).wait_recv()
        step = 3 if way else 1
        total = mine(half, step, way)[...].astype(F32) + relay_in[half][way].astype(F32)
        relay_out[half][way] = total.astype(BF16)
        near_go(half, way, 2).start()

    def last_go(half, db):
        b = x_b(half, db)
        return remote(
            last_out[half].at[b], last_in[half].at[db - 1], last_send.at[half, db - 1], last_recv.at[half, db - 1],
            b_device(half, db),
        )

    def gather_near(half):
        for way in range(2):
            near_go(half, way, 1).wait_recv()
            near_go(half, way, 2).wait_recv()
        for part in range(2):
            total = mine(half, 0, part)[...].astype(F32)
            for way in range(2):
                total = total + near_in[half][way, part].astype(F32)
            last_sum[half][pl.ds(2 * part, 2)] = total
            last_out[half][pl.ds(2 * part, 2)] = total.astype(BF16)
        for db in (2, 1, 3):
            last_go(half, db).start()

    odd = lax.rem(p.x, 2)
    mate = p.x + 1 - 2 * odd
    far, far_mate = lax.rem(p.x + 2, 4), lax.rem(mate + 2, 4)
    far_part = lax.div(far, 2)

    def near_part(part):
        near_go(0, part, 0).start()
        near_go(0, 1 - part, 1).start()

    out_blocks(far)
    out_blocks(far_mate)
    add_blocks(far)
    near_go(1, 0, 0).start()
    near_go(1, 1, 0).start()
    out_blocks(mate)
    add_blocks(far_mate)
    for value in range(2):
        @pl.when(odd == value)
        def _():
            near_go(1, 1 - value, 1).start()

        @pl.when(far_part == value)
        def _():
            near_part(value)

    out_blocks(p.x)
    add_blocks(mate)
    for value in range(2):
        @pl.when(odd == value)
        def _():
            near_go(1, value, 1).start()

    relay(1, 0)
    relay(1, 1)
    add_blocks(p.x)
    for value in range(2):
        @pl.when(far_part == value)
        def _():
            near_part(1 - value)

    for c in range(2):
        for zl in range(2):
            row = jnp.sum(jnp.transpose(dot_acc[zl, c]), axis=0, keepdims=True)
            dots[0, c, zl] = jnp.broadcast_to(row, (8, 128))

    def dot_go(slot, src, dst, device):
        return remote(src, dst, dot_send.at[slot], dot_recv.at[slot], device)

    first_dot = dot_go(0, dots.at[0, 1 - p.c], dots.at[1, 0], p.at(dc=1))
    first_dot.start()
    relay(0, 0)
    relay(0, 1)
    first_dot.wait_recv()
    for zl in range(2):
        dots[1, 1, zl] = dots[0, p.c, zl] + dots[1, 0, zl]
    z_dots = [
        dot_go(dz, dots.at[1, 1, lax.rem(p.zl + dz, 2)], dots.at[2, lax.div(dz, 2), dz % 2], p.at(dz=dz))
        for dz in (1, 2, 3)
    ]
    for copy in z_dots:
        copy.start()
    gather_near(1)
    for copy in z_dots:
        copy.wait_recv()
    dots[3, 0, 0] = (dots[1, 1, p.zl] + dots[2, 0, 1]) + (dots[2, 1, 0] + dots[2, 1, 1])
    x_dots = [
        dot_go(3 + dx, dots.at[3, 0, 0], dots.at[4, dx // 2, dx % 2], p.at(dx=dx)) for dx in (1, 2, 3)
    ]
    for copy in x_dots:
        copy.start()
    gather_near(0)
    for copy in x_dots:
        copy.wait_recv()
    dot = (dots[3, 0, 0] + dots[4, 0, 1]) + (dots[4, 1, 0] + dots[4, 1, 1])
    dot = jnp.transpose(jnp.broadcast_to(dot[:1], (128, 128)))[:, :1] * (1.0 / OUT_COLS)
    inverse = inv_ref[p.zl, p.c][:, :1]
    slope = inverse * inverse * inverse * dot
    for half in (1, 0):
        for db in (1, 2, 3):
            last_go(half, db).wait_recv()
        b = p.z if half else p.x
        total = last_sum[half][b] + last_in[half][0].astype(F32)
        total = total + (last_in[half][1].astype(F32) + last_in[half][2].astype(F32))
        rows = slice(SUM_ROWS[half][0], sum(SUM_ROWS[half]))
        own = x_all[p.zl, p.c, p.x, p.zh, rows].astype(F32)
        out[rows] = inverse[rows] * total - own * slope[rows]

    for x in range(4):
        for zh in range(2):
            swap(x, zh).wait_send()
    for half in halves:
        for way in range(2):
            for kind in range(3):
                near_go(half, way, kind).wait_send()
        for db in (1, 2, 3):
            last_go(half, db).wait_send()
    for copy in [first_dot] + z_dots + x_dots:
        copy.wait_send()

    for piece in range(3):
        for slot in range(9):
            ref = w_of(piece).at[0] if slot < 3 else w_part(piece, 0, 0)
            remote(ref, ref, w_send.at[piece, slot], w_recv.at[piece, 0], p.at(dc=1)).wait_send()
    for half in halves:
        for slot in range(19):
            ref = x_piece(half, 0, 0) if slot < 15 else x_full(half, 0, 0)
            remote(ref, ref, x_send.at[half, slot], x_core.at[half, 0], p.at(dc=1)).wait_send()
    for slot in range(6):
        ref = gains.at[0] if slot < 3 else gain_y
        remote(ref, ref, gain_send.at[slot], gain_recv.at[0], p.at(dc=1)).wait_send()
    for i in range(3):
        remote(g_all.at[0], g_all.at[0], g_send.at[i], g_recv.at[0], p.at(dc=1)).wait_send()
    for dy in (1, 2, 3):
        @pl.when(p.y + dy < 4)
        def _():
            remote(own_kv, own_kv, kv_send.at[dy - 1], kv_recv.at[p.c, p.y], p.at(dc=1)).wait_send()

    for dy in (0, 1, 2, 3):
        @pl.when(p.y >= dy)
        def _():
            remote(own_kv, own_kv, kv_send.at[3 + dy], kv_recv.at[p.c, p.y], p.at(dc=1)).wait_send()

    @pl.loop(0, p.y)
    def _(block):
        core_go(block).wait_send()
        back_go(block).wait_send()

    core_go(p.y).wait_send()


def body(trunk_out, norm_gain, w_query, w_key, value_weight, context_gradient):
    dma, vmem = pltpu.SemaphoreType.DMA, pltpu.VMEM
    halves = []
    for _, rows in SUM_ROWS:
        halves += [
            vmem((2, 2, rows, 512), BF16),
            vmem((2, 2, rows, 512), BF16),
            vmem((2, 2, 2, rows, 512), BF16),
            vmem((4, rows, 512), F32),
            vmem((4, rows, 512), BF16),
            vmem((3, rows, 512), BF16),
        ]
    return pl.pallas_call(
        backward_kernel,
        out_shape=jax.ShapeDtypeStruct((128, 512), F32),
        in_specs=[ANY, pl.BlockSpec(memory_space=pltpu.VMEM)] + [ANY] * 4,
        out_specs=pl.BlockSpec(memory_space=pltpu.VMEM),
        scratch_shapes=[
            vmem((256, 2048), BF16),
            vmem((256, 256), BF16),
            vmem((256, 256), BF16),
            vmem((128, 2048), BF16),
            vmem((4, 256, 128), BF16),
            vmem((2, 4, 256, 256), BF16),
            vmem((4, 128, Q_COLS), BF16),
            vmem((2, 2, 4, 2, 128, 512), BF16),
            vmem((16, 256, 128), BF16),
            vmem((2, 16, 256, 256), BF16),
            vmem((2, 2, 128, W_COLS), BF16),
            vmem((2, 2, 128, 128), F32),
            vmem((16, 16, 256), BF16),
            vmem((8, 8, 512), F32),
            vmem((8, ROWS, 512), BF16),
            vmem((4, ROWS, HEAD_SIZE), BF16),
            vmem((4, 128, Q_COLS), BF16),
            vmem((2, 4, ROWS, HEAD_SIZE), BF16),
            vmem((4, HEAD_SIZE, ROWS), BF16),
            vmem((4, HEAD_SIZE, ROWS), BF16),
            vmem((2, HEAD_SIZE, ROWS), BF16),
            vmem((2 * ROWS, HEAD_SIZE), BF16),
            vmem((2, 2, 4, ROWS, ROWS), F32),
            vmem((2, 4, 8, ROWS), F32),
            vmem((2, HEAD_SIZE, ROWS), F32),
            vmem((4, ROWS, HEAD_SIZE), F32),
            vmem((4, ROWS, HEAD_SIZE), F32),
            vmem((2, 4, ROWS, HEAD_SIZE), BF16),
            vmem((4, ROWS, HEAD_SIZE), BF16),
            vmem((4, ROWS, HEAD_SIZE), BF16),
            vmem((2, 2, 128, 128), F32),
            vmem((4, 2, 2, 128, 512), BF16),
            vmem((5, 2, 2, 8, 128), F32),
            *halves,
            dma((3, 9)), dma((3, 4)), dma((3, 4, 2)),
            dma((2, 19)), dma((2, 4, 4)), dma((2, 4)),
            dma((6,)), dma((4,)), dma((4,)),
            dma((3,)), dma((4,)),
            dma((7,)), dma((2, 4)),
            dma((4,)), dma((4,)), dma((4,)), dma((4,)),
            dma((8,)),
            dma((4, 2)), dma((4, 2)),
            dma((2, 2, 3)), dma((2, 2, 3)),
            dma((2, 3)), dma((2, 3)),
            dma((7,)), dma((7,)),
        ],
        compiler_params=pltpu.CompilerParams(
            collective_id=0, has_side_effects=True, vmem_limit_bytes=60 * 1024 * 1024
        ),
        name="attention_block_backward",
    )(trunk_out, norm_gain, w_query, w_key, value_weight, context_gradient)


def solution(mesh):
    placed = (
        P("ctx", ("grp", "tp")),
        P("grp", "ctx"),
        P("grp", "ctx", "tp"),
        P("grp", "ctx", "tp"),
        P("grp", "ctx", "tp"),
        P("grp", "ctx", "tp"),
    )
    return jax.shard_map(
        body, mesh=mesh, in_specs=placed, out_specs=P("ctx", ("grp", "tp")), check_vma=False
    )
```

```python
import jax
import jax.numpy as jnp
from jax import lax
from jax.experimental import pallas as pl
from jax.experimental.pallas import tpu as pltpu
from jax.sharding import PartitionSpec as P

HEAD_SIZE = 128
EPSILON = 1e-05
MASKED_SCORE = -1e30
LOG2E = 1.4426950408889634
MESH = pl.DeviceIdType.MESH
ANY = pl.BlockSpec(memory_space=pl.ANY)
BF16 = jnp.bfloat16
F32 = jnp.float32
ROWS = 512
OUT_COLS = 4096
Q_COLS = 512
W_COLS = 640


class Place:
    def __init__(self):
        self.x = lax.axis_index("grp")
        ctx = lax.axis_index("ctx")
        self.ctx = ctx
        self.zh = lax.axis_index("tp")
        self.y = lax.div(ctx, 4)
        self.j = lax.rem(ctx, 4)
        self.zl = lax.div(self.j, 2)
        self.c = lax.rem(ctx, 2)
        self.z = self.zh * 2 + self.zl
        self.known = {}
        for dc in range(2):
            self.keep(dc=dc)
            self.keep(dzl=1, dc=dc)
        for d in range(1, 4):
            self.keep(dx=d)
            self.keep(dy=d)
            self.keep(dz=d)

    def keep(self, **deltas):
        deltas = {key: value for key, value in deltas.items() if value}
        self.known[tuple(sorted(deltas.items()))] = self.work_out(**deltas)

    def at(self, **deltas):
        deltas = {key: value for key, value in deltas.items() if not isinstance(value, int) or value}
        key = tuple(sorted(deltas.items()))
        return self.known[key] if key in self.known else self.work_out(**deltas)

    def work_out(self, dx=0, dy=0, dzl=0, dc=0, dz=0):
        def moved(value, step, size):
            return value if isinstance(step, int) and step == 0 else lax.rem(value + step, size)

        x, y, c = moved(self.x, dx, 4), moved(self.y, dy, 4), moved(self.c, dc, 2)
        zl, zh = moved(self.zl, dzl, 2), self.zh
        if dz:
            z = moved(self.z, dz, 4)
            zl, zh = lax.rem(z, 2), lax.div(z, 2)
        return {"grp": x, "ctx": y * 4 + zl * 2 + c, "tp": zh}


def greet(place, partners):
    barrier = pltpu.get_barrier_semaphore()
    for partner in partners:
        pl.semaphore_signal(barrier, inc=1, device_id=place.at(**partner), device_id_type=MESH)
    pl.semaphore_wait(barrier, len(partners))


def remote(src, dst, send_sem, recv_sem, device):
    return pltpu.make_async_remote_copy(
        src_ref=src, dst_ref=dst, send_sem=send_sem, recv_sem=recv_sem, device_id=device, device_id_type=MESH
    )


J_OTHERS = [dict(dc=1), dict(dzl=1), dict(dzl=1, dc=1)]
PARTNERS = J_OTHERS + [{axis: d} for axis in ("dx", "dy", "dz") for d in (1, 2, 3)]
GATHER_ROWS = ((0, 96), (96, 32))
SUM_FEATURES = ((0, 192), (192, 320))


def mm(a, b, contract):
    return lax.dot_general(a, b, ((contract[:1], contract[1:]), ((), ())), preferred_element_type=F32)


def go(src, dst, send_sem, recv_sem, device):
    remote(src, dst, send_sem, recv_sem, device).start()


def arrived(ref, sem):
    pltpu.make_async_copy(ref, ref, sem).wait()


def lanes(index, width=128):
    return pl.ds(pl.multiple_of(index * width, width), width)


def backward_kernel(
    trunk, gain, wq, wk, wv, grads,
    out,
    wq_in, wk_in, wv_in, g_in, kv_cut, q_cut, g_cut,
    x_all, w_kv, w_q, d_turned, inv_ref, inv_rows, own_turned, gains, gain_rows, normed, q_all, g_all, kv, kt, q_turned, g_turned, g_pair, tiles, tops, dq_ref, dk_ref, dv_ref,
    dkv, core_in, back,
    sums, dots,
    relay_in_0, relay_out_0, near_in_0, last_sum_0, last_out_0, last_in_0,
    relay_in_1, relay_out_1, near_in_1, last_sum_1, last_out_1, last_in_1,
    w_send, w_recv, w_set, x_send, x_recv, x_core, gain_send, gain_recv, gain_set, g_send, g_recv,
    kv_send, kv_recv, core_send, core_recv, back_send, back_recv, local,
    swap_send, swap_recv, near_send, near_recv, last_send, last_recv, dot_send, dot_recv,
):
    relay_in, relay_out, near_in = (relay_in_0, relay_in_1), (relay_out_0, relay_out_1), (near_in_0, near_in_1)
    last_sum, last_out, last_in = (last_sum_0, last_sum_1), (last_out_0, last_out_1), (last_in_0, last_in_1)
    p = Place()
    pairs = ((wk.at[0], wk_in), (wv.at[0], wv_in), (wq.at[0], wq_in), (grads.at[0], g_in))
    loads = [pltpu.make_async_copy(src, dst, local.at[i]) for i, (src, dst) in enumerate(pairs)]
    for load in loads:
        load.start()
    greet(p, PARTNERS)

    def j_of(dzl=0, dc=0):
        return lax.rem(p.zl + dzl, 2) * 2 + lax.rem(p.c + dc, 2)

    below, above, across = [lax.rem(p.y + d, 4) for d in (3, 1, 2)]
    j_others = [(j_of(**other), p.at(**other)) for other in J_OTHERS]

    def w_of(piece):
        return w_q.at[piece - 1] if piece else w_kv

    def w_cut(piece):
        return q_cut.at[piece - 1] if piece else kv_cut

    def w_stage(piece):
        cut, ref = w_cut(piece), w_of(piece)
        for j in range(4):
            if piece:
                column = j * Q_COLS + (piece - 1) * 256
                cut[j] = wq_in[:, column : column + 256]
            else:
                cut[j] = (wv_in if j % 2 else wk_in)[:, 128 * (j // 2) : 128 * (j // 2) + 128]
        ref[p.ctx] = cut[p.j]

    def w_leave(piece, partners=(0, 1, 2)):
        cut, ref = w_cut(piece), w_of(piece)
        for i in partners:
            j, device = j_others[i]
            go(cut.at[j], ref.at[p.ctx], w_send.at[piece, i], w_recv.at[piece, p.j], device)

    def w_part(piece, y, part):
        return w_of(piece).at[pl.ds(4 * y + 2 * part, 2)]

    def w_go(piece, y, part, slot, device):
        ref = w_part(piece, y, part)
        go(ref, ref, w_send.at[piece, slot], w_set.at[piece, y, part], device)

    def w_wait(piece, y, part):
        arrived(w_part(piece, y, part), w_set.at[piece, y, part])

    def w_near(piece):
        j, _ = j_others[0]
        arrived(w_of(piece).at[p.y * 4 + j], w_recv.at[piece, j])
        w_go(piece, p.y, p.zl, 3, p.at(dy=1))
        w_go(piece, p.y, p.zl, 4, p.at(dy=3))

    def w_far(piece):
        for j, _ in j_others[1:]:
            arrived(w_of(piece).at[p.y * 4 + j], w_recv.at[piece, j])
        w_go(piece, p.y, 1 - p.zl, 5, p.at(dy=1))
        w_go(piece, p.y, 1 - p.zl, 6, p.at(dy=3))

    def w_relay(piece):
        w_wait(piece, below, 0)
        w_go(piece, below, 0, 7, p.at(dy=1))
        w_wait(piece, above, 1)
        w_go(piece, above, 1, 8, p.at(dy=3))

    def x_a(half, d):
        return lax.rem((p.x if half else p.z) + d, 4)

    def x_b(half, d):
        return lax.rem((p.z if half else p.x) + d, 4)

    def a_device(half, da):
        return p.at(dx=da) if half else p.at(dz=da)

    def b_device(half, db):
        return p.at(dz=db) if half else p.at(dx=db)

    def x_piece(half, x, z):
        return x_all.at[lax.rem(z, 2), p.c, x, lax.div(z, 2), pl.ds(*GATHER_ROWS[half])]

    def x_full(half, b, c):
        if half:
            return x_all.at[lax.rem(b, 2), c, :, lax.div(b, 2), pl.ds(*GATHER_ROWS[1])]
        return x_all.at[:, c, b, :, pl.ds(*GATHER_ROWS[0])]

    def x_at(half, da, db):
        a, b = x_a(half, da), x_b(half, db)
        return (x_piece(1, a, b) if half else x_piece(0, b, a)), x_recv.at[half, a, b]

    def x_go(half, da, db, slot, device, src=None):
        dst, sem = x_at(half, da, db)
        go(dst if src is None else src, dst, x_send.at[half, slot], sem, device)

    def x_first(half):
        own = trunk.at[pl.ds(*GATHER_ROWS[half])]
        for i, d in enumerate((2, 1, 3)):
            x_go(half, 0, 0, i, a_device(half, d), own)
        x_go(half, 0, 0, 3, b_device(half, 1), own)
        x_go(half, 0, 0, 4, b_device(half, 3), own)

    def x_second(half):
        for i, d in enumerate((1, 3, 2)):
            arrived(*x_at(half, d, 0))
            x_go(half, d, 0, 5 + 2 * i, b_device(half, 1))
            x_go(half, d, 0, 6 + 2 * i, b_device(half, 3))

    def x_relay(half):
        for i in range(2):
            arrived(*x_at(half, i, 3))
            x_go(half, i, 3, 11 + 2 * i, b_device(half, 1))
            arrived(*x_at(half, 2 + i, 1))
            x_go(half, 2 + i, 1, 12 + 2 * i, b_device(half, 3))

    def x_to_core(half, d):
        b = x_b(half, d)
        ref = x_full(half, b, p.c)
        go(ref, ref, x_send.at[half, 15 + d], x_core.at[half, b], p.at(dc=1))

    halves = (0, 1)
    for half in halves:
        x_first(half)
    loads[0].wait()
    loads[1].wait()
    w_stage(0)
    w_leave(0)
    own_x = x_all.at[p.zl, p.c, p.x, p.zh]
    pltpu.make_async_copy(trunk, own_x, local.at[5]).start()
    gains[p.ctx] = jnp.broadcast_to(gain[...], (16, 256))
    for i, (j, device) in enumerate(j_others):
        go(gains.at[p.ctx], gains.at[p.ctx], gain_send.at[i], gain_recv.at[p.j], device)
    loads[2].wait()
    w_stage(1)
    w_stage(2)
    w_leave(1, (0,))
    w_near(0)
    w_near(1)
    for half in halves:
        x_second(half)
    w_leave(1, (1, 2))
    w_far(0)
    pltpu.make_async_copy(own_x, own_x, local.at[5]).wait()
    for half in halves:
        x_to_core(half, 0)
    for half in halves:
        x_relay(half)
    for j, _ in j_others:
        arrived(gains.at[p.y * 4 + j], gain_recv.at[j])
    gain_y = gains.at[pl.ds(4 * p.y, 4)]
    for dy in (1, 2, 3):
        go(gain_y, gain_y, gain_send.at[2 + dy], gain_set.at[p.y], p.at(dy=dy))
    w_far(1)
    w_relay(0)
    own_turned[...] = jnp.transpose(own_x[...].astype(F32))
    for half in halves:
        for i in range(2):
            arrived(*x_at(half, 2 + i, 3))
            arrived(*x_at(half, i, 1))
        x_to_core(half, 3)
        x_to_core(half, 1)
    w_leave(2)
    for half in halves:
        for i in range(4):
            arrived(*x_at(half, i, 2))
        x_to_core(half, 2)
    loads[3].wait()
    for j in range(4):
        g_cut[j] = g_in[:, Q_COLS * j : Q_COLS * j + Q_COLS]
    for i, (j, device) in enumerate(j_others):
        go(g_cut.at[j], g_all.at[p.j], g_send.at[i], g_recv.at[p.j], device)
    g_all[p.j] = g_cut[p.j]
    w_near(2)
    for d in (1, 2, 3):
        y = lax.rem(p.y + d, 4)
        arrived(gains.at[pl.ds(4 * y, 4)], gain_set.at[y])
    for block in range(8):
        row = jnp.concatenate([gains[2 * block][:1], gains[2 * block + 1][:1]], axis=1)
        gain_rows[block] = jnp.broadcast_to(row.astype(F32), (8, 512))
    gain_columns = wq_in

    @pl.loop(0, 8)
    def _(block):
        turned = jnp.transpose(jnp.broadcast_to(gain_rows[block][:1], (128, 512))).astype(BF16)
        gain_columns[:, lanes(2 * block)] = turned[:256]
        gain_columns[:, lanes(2 * block + 1)] = turned[256:]

    for half in halves:
        for b in range(4):
            arrived(x_full(half, b, 1 - p.c), x_core.at[half, b])

    def norm_rows(step):
        group = lax.div(step, 4)
        rows = pl.ds(pl.multiple_of(lax.rem(step, 4) * 32, 32), 32)
        zl, c = lax.div(group, 2), lax.rem(group, 2)
        total = jnp.zeros((32, 128), F32)
        for block in range(8):
            part = x_all[zl, c, block // 2, block % 2, rows].astype(F32)
            part = part * part
            total = total + ((part[:, :128] + part[:, 128:256]) + (part[:, 256:384] + part[:, 384:]))
        inverse = lax.rsqrt(jnp.sum(total, axis=1, keepdims=True) * (1.0 / OUT_COLS) + EPSILON)
        inverse = jnp.broadcast_to(inverse, (32, 128))
        inv_ref[zl, c, rows] = inverse
        wide = jnp.concatenate([inverse] * 4, axis=1)
        for block in range(8):
            scaled = x_all[zl, c, block // 2, block % 2, rows].astype(F32) * wide
            scaled = scaled.reshape(4, 8, 512) * gain_rows[block][None]
            row = pl.ds(pl.multiple_of(step * 32, 32), 32)
            normed[block, row] = scaled.reshape(32, 512).astype(BF16)

    def project(piece):
        ref, width = w_of(piece), 256 if piece else 128

        def part(y):
            left = jnp.concatenate([normed[2 * y], normed[2 * y + 1]], axis=1)
            return jnp.dot(left, ref[pl.ds(4 * y, 4)].reshape(1024, width), preferred_element_type=F32)

        total = part(p.y)
        w_wait(piece, below, 1)
        total = total + part(below)
        w_wait(piece, above, 0)
        total = total + part(above)
        w_wait(piece, across, 0)
        w_wait(piece, across, 1)
        return (total + part(across)).astype(BF16)

    def project_heads(piece):
        q = project(piece)
        for i in range(2):
            q_all[2 * piece - 2 + i] = q[:, 128 * i : 128 * i + 128]
            q_turned[2 * piece - 2 + i] = jnp.transpose(q[:, 128 * i : 128 * i + 128])

    @pl.loop(0, 8)
    def _(step):
        norm_rows(step)

    w_relay(1)

    @pl.loop(8, 16)
    def _(step):
        norm_rows(step)

    kv[p.c, p.y] = project(0)
    own_kv = kv.at[p.c, p.y]
    for dy in (1, 2, 3):
        @pl.when(p.y + dy < 4)
        def _():
            go(own_kv, own_kv, kv_send.at[dy - 1], kv_recv.at[p.c, p.y], p.at(dy=dy))

    go(own_kv, own_kv, kv_send.at[3], kv_recv.at[p.c, p.y], p.at(dc=1))
    w_far(2)
    for zl in range(2):
        for c in range(2):
            inv_rows[zl, c] = jnp.transpose(inv_ref[zl, c])[:8]
    project_heads(1)
    for dy in (1, 3, 2):
        @pl.when(p.y >= dy)
        def _():
            ref = kv.at[p.c, p.y - dy]
            arrived(ref, kv_recv.at[p.c, p.y - dy])
            go(ref, ref, kv_send.at[3 + dy], kv_recv.at[p.c, p.y - dy], p.at(dc=1))

    for j, _ in j_others:
        arrived(g_all.at[j], g_recv.at[j])
    for dy in (0, 1, 3, 2):
        @pl.when(p.y >= dy)
        def _():
            arrived(kv.at[1 - p.c, p.y - dy], kv_recv.at[1 - p.c, p.y - dy])

    scale = HEAD_SIZE ** -0.5
    factor = scale * LOG2E
    dk_ref[...] = jnp.zeros_like(dk_ref)
    dv_ref[...] = jnp.zeros_like(dv_ref)

    @pl.loop(0, p.y + 1)
    def _(block):
        kt[block] = jnp.transpose(kv[0, block])

    def fold(value, combine):
        parts = [value[8 * i : 8 * i + 8] for i in range(4)]
        return combine(combine(parts[0], parts[1]), combine(parts[2], parts[3]))

    def over(row, count):
        return jnp.broadcast_to(row, (count, ROWS))

    def statistics(head, block, s, t, state, diagonal):
        top, total, delta = state
        tiles[head, 1, block] = t
        parts = [s[32 * i : 32 * i + 32] for i in range(16)]
        if diagonal:
            key = lax.broadcasted_iota(jnp.int32, (32, ROWS), 0)
            row = lax.broadcasted_iota(jnp.int32, (32, ROWS), 1)
            parts = [jnp.where(key <= row - 32 * i, part, MASKED_SCORE) for i, part in enumerate(parts)]
        most = fold(parts[0], jnp.maximum)
        for part in parts[1:]:
            most = jnp.maximum(most, fold(part, jnp.maximum))
        now = jnp.maximum(top, jnp.max(most, axis=0, keepdims=True))
        tops[head, block] = over(now, 8)
        wide = over(now, 32)
        sums = jnp.zeros((8, ROWS), F32)
        deltas = jnp.zeros((8, ROWS), F32)
        for i, part in enumerate(parts):
            e = jnp.exp2((part - wide) * factor)
            tiles[head, 0, block, 32 * i : 32 * i + 32] = e
            sums = sums + fold(e, jnp.add)
            deltas = deltas + fold(e * t[32 * i : 32 * i + 32], jnp.add)
        shrink = jnp.exp2((top - now) * factor)
        total = total * shrink + jnp.sum(sums, axis=0, keepdims=True)
        delta = delta * shrink + jnp.sum(deltas, axis=0, keepdims=True)
        return now, total, delta

    def scores(pair, block, states, diagonal):
        products = []
        for head in range(2):
            s = mm(kv[0, block], q_turned[2 * pair + head], (1, 0))
            products.append((s, mm(kv[1, block], g_turned[head], (1, 0))))
        return tuple(statistics(i, block, *products[i], states[i], diagonal) for i in range(2))

    def lows(head, block, stats):
        top, inverse, delta = stats
        weight = over(jnp.exp2((tops[head, block][:1] - top) * factor) * inverse, 32)
        wide = over(delta, 32)
        probs_low, ds_low = [], []
        for i in range(16):
            chunk = pl.ds(32 * i, 32)
            probs = tiles[head, 0, block, chunk] * weight
            probs_low.append(probs.astype(BF16))
            ds_low.append((probs * (tiles[head, 1, block, chunk] - wide)).astype(BF16))
        return jnp.concatenate(probs_low, axis=0), jnp.concatenate(ds_low, axis=0)

    def pair_grads(pair, block, stats):
        both = [lows(head, block, stats[head]) for head in range(2)]
        for head in range(2):
            dq_ref[head] += mm(kt[block], both[head][1], (1, 0))
        probs = jnp.concatenate([both[0][0], both[1][0]], axis=1)
        ds = jnp.concatenate([both[0][1], both[1][1]], axis=1)
        dv_ref[block] += mm(probs, g_pair[...], (1, 0))
        dk_ref[block] += mm(ds, q_all[pl.ds(2 * pair, 2)].reshape(2 * ROWS, HEAD_SIZE), (1, 0))

    def core_go(block):
        return remote(dkv.at[1 - p.c, block], core_in.at[block], core_send.at[block], core_recv.at[block], p.at(dc=1))

    def back_go(block):
        device = {"grp": p.x, "ctx": block * 4 + p.j, "tp": p.zh}
        return remote(dkv.at[p.c, block], back.at[p.y], back_send.at[block], back_recv.at[p.y], device)

    def to_core(block):
        dkv[0, block] = (dk_ref[block] * scale).astype(BF16)
        dkv[1, block] = dv_ref[block].astype(BF16)
        core_go(block).start()

    def to_rows(block):
        core_go(block).wait_recv()
        dkv[p.c, block] = (dkv[p.c, block].astype(F32) + core_in[block].astype(F32)).astype(BF16)
        back_go(block).start()

    @pl.loop(0, 2)
    def _(pair):
        @pl.when(pair == 1)
        def _():
            project_heads(2)

        for head in range(2):
            g = g_all[:, :, lanes(2 * pair + head)].reshape(ROWS, HEAD_SIZE)
            g_pair[ROWS * head : ROWS * head + ROWS] = g
            g_turned[head] = jnp.transpose(g)
        dq_ref[...] = jnp.zeros_like(dq_ref)
        start = (jnp.full((1, ROWS), MASKED_SCORE, F32), jnp.zeros((1, ROWS), F32), jnp.zeros((1, ROWS), F32))
        states = lax.fori_loop(0, p.y, lambda block, now: scores(pair, block, now, False), (start, start))
        states = scores(pair, p.y, states, True)

        @pl.when(pair == 0)
        def _():
            w_relay(2)

        stats = []
        for top, total, delta in states:
            inverse = 1.0 / total
            stats.append((top, inverse, delta * inverse))

        @pl.loop(0, p.y + 1)
        def _(block):
            pair_grads(pair, block, stats)

            @pl.when(pair == 1)
            def _():
                to_core(block)

                @pl.when(block > 0)
                def _():
                    to_rows(block - 1)

        for head in range(2):
            d_turned[2 * pair + head + 1] = (dq_ref[head] * scale).astype(BF16)

    core_go(p.y).wait_recv()
    dk_ref[0] = dkv[p.c, p.y].astype(F32) + core_in[p.y].astype(F32)
    for dy in (1, 2, 3):
        @pl.when(p.y + dy < 4)
        def _():
            arrived(back.at[p.y + dy], back_recv.at[p.y + dy])
            dk_ref[0] += back[p.y + dy].astype(F32)
    d_turned[0] = jnp.transpose(dk_ref[0]).astype(BF16)

    dot = jnp.zeros((8, ROWS), F32)
    own_turned_kv = jnp.transpose(kv[p.c, p.y])
    for i in range(5):
        for k in range(0, 128, 32):
            turned = q_turned[i - 1, k : k + 32] if i else own_turned_kv[k : k + 32]
            dot = dot + fold(d_turned[i, k : k + 32].astype(F32) * turned.astype(F32), jnp.add)
    dot = jnp.sum(dot, axis=0, keepdims=True)
    for zl in range(2):
        for c in range(2):
            group = zl * 2 + c
            dots[0, c, zl] = jnp.broadcast_to(dot[:, 128 * group : 128 * group + 128], (8, 128)) / inv_rows[zl, c]

    def out_block(x, zh):
        block = x * 2 + zh
        left = [w_of(piece)[pl.ds(2 * block, 2)].reshape(512, 256 if piece else 128) for piece in range(3)]
        part = mm(jnp.concatenate(left, axis=1), d_turned[...].reshape(W_COLS, ROWS), (1, 0))
        for i in range(16):
            rows = slice(32 * i, 32 * i + 32)
            gain_column = gain_columns[32 * (i % 8) : 32 * (i % 8) + 32, lanes(2 * block + i // 8)].astype(F32)
            tiles[zh, 0, x, rows] = part[rows] * jnp.concatenate([gain_column] * 4, axis=1)
        for zl in range(2):
            for i in range(8):
                rows = slice(64 * i, 64 * i + 64)
                normed[block, swap_rows(i), swap_lanes(zl, i)] = tiles[zh, 0, x, rows, lanes(zl * 2 + 1 - p.c)].astype(BF16)

    def swap_rows(i, first=0):
        return slice(first + 64 * (i % 4), first + 64 * (i % 4) + 64)

    def swap_lanes(zl, i):
        first = 128 * (2 * zl + i // 4)
        return slice(first, first + 128)

    def swap_out(x, zh):
        return normed.at[2 * x + zh, pl.ds(0, 256)]

    def swap_in(x, zh):
        return normed.at[2 * x + zh, pl.ds(256, 256)]

    def swap(x, zh):
        return remote(swap_out(x, zh), swap_in(x, zh), swap_send.at[x, zh], swap_recv.at[x, zh], p.at(dc=1))

    def out_blocks(x):
        @pl.loop(0, 2)
        def _(zh):
            out_block(x, zh)
            swap(x, zh).start()

    def add_blocks(x):
        @pl.loop(0, 2)
        def _(zh):
            swap(x, zh).wait_recv()
            for zl in range(2):
                for i in range(8):
                    rows = slice(64 * i, 64 * i + 64)
                    other = normed[2 * x + zh, swap_rows(i, 256), swap_lanes(zl, i)].astype(F32)
                    sums[x, zh, zl, rows] = (tiles[zh, 0, x, rows, lanes(zl * 2 + p.c)] + other).astype(BF16)

    def mine(half, da, part):
        a = x_a(half, da)
        if half:
            return sums.at[a, part, :, pl.ds(*SUM_FEATURES[1])]
        return sums.at[pl.ds(2 * part, 2), lax.div(a, 2), lax.rem(a, 2), pl.ds(*SUM_FEATURES[0])]

    def near_go(half, way, kind):
        step = 3 if way else 1
        if kind == 0:
            src, dst = mine(half, 2, way), relay_in[half].at[way]
        elif kind == 1:
            src, dst = mine(half, step, 1 - way), near_in[half].at[way, 1 - way]
        else:
            src, dst = relay_out[half].at[way], near_in[half].at[way, way]
        return remote(src, dst, near_send.at[half, way, kind], near_recv.at[half, way, kind], a_device(half, step))

    def relay(half, way):
        near_go(half, way, 0).wait_recv()
        step = 3 if way else 1
        total = mine(half, step, way)[...].astype(F32) + relay_in[half][way].astype(F32)
        relay_out[half][way] = total.astype(BF16)
        near_go(half, way, 2).start()

    def last_go(half, db):
        b = x_b(half, db)
        return remote(
            last_out[half].at[b], last_in[half].at[db - 1], last_send.at[half, db - 1], last_recv.at[half, db - 1],
            b_device(half, db),
        )

    def gather_near(half):
        for way in range(2):
            near_go(half, way, 1).wait_recv()
            near_go(half, way, 2).wait_recv()
        for part in range(2):
            total = mine(half, 0, part)[...].astype(F32)
            for way in range(2):
                total = total + near_in[half][way, part].astype(F32)
            last_sum[half][pl.ds(2 * part, 2)] = total
            last_out[half][pl.ds(2 * part, 2)] = total.astype(BF16)
        for db in (2, 1, 3):
            last_go(half, db).start()

    odd = lax.rem(p.x, 2)
    mate = p.x + 1 - 2 * odd
    far, far_mate = lax.rem(p.x + 2, 4), lax.rem(mate + 2, 4)
    far_part = lax.div(far, 2)

    def near_part(part):
        near_go(0, part, 0).start()
        near_go(0, 1 - part, 1).start()

    out_blocks(far)
    out_blocks(far_mate)
    add_blocks(far)
    near_go(1, 0, 0).start()
    near_go(1, 1, 0).start()
    out_blocks(mate)
    add_blocks(far_mate)
    for value in range(2):
        @pl.when(odd == value)
        def _():
            near_go(1, 1 - value, 1).start()

        @pl.when(far_part == value)
        def _():
            near_part(value)

    out_blocks(p.x)
    add_blocks(mate)
    for value in range(2):
        @pl.when(odd == value)
        def _():
            near_go(1, value, 1).start()

    relay(1, 0)
    relay(1, 1)
    add_blocks(p.x)
    for value in range(2):
        @pl.when(far_part == value)
        def _():
            near_part(1 - value)

    def dot_go(slot, src, dst, device):
        return remote(src, dst, dot_send.at[slot], dot_recv.at[slot], device)

    first_dot = dot_go(0, dots.at[0, 1 - p.c], dots.at[1, 0], p.at(dc=1))
    first_dot.start()
    relay(0, 0)
    relay(0, 1)
    first_dot.wait_recv()
    for zl in range(2):
        dots[1, 1, zl] = dots[0, p.c, zl] + dots[1, 0, zl]
    z_dots = [
        dot_go(dz, dots.at[1, 1, lax.rem(p.zl + dz, 2)], dots.at[2, lax.div(dz, 2), dz % 2], p.at(dz=dz))
        for dz in (1, 2, 3)
    ]
    for copy in z_dots:
        copy.start()
    gather_near(1)
    for copy in z_dots:
        copy.wait_recv()
    dots[3, 0, 0] = (dots[1, 1, p.zl] + dots[2, 0, 1]) + (dots[2, 1, 0] + dots[2, 1, 1])
    x_dots = [
        dot_go(3 + dx, dots.at[3, 0, 0], dots.at[4, dx // 2, dx % 2], p.at(dx=dx)) for dx in (1, 2, 3)
    ]
    for copy in x_dots:
        copy.start()
    gather_near(0)
    for copy in x_dots:
        copy.wait_recv()
    dot = (dots[3, 0, 0] + dots[4, 0, 1]) + (dots[4, 1, 0] + dots[4, 1, 1])
    inverse = inv_rows[p.zl, p.c][:1]
    slope = inverse * inverse * inverse * dot[:1] * (1.0 / OUT_COLS)
    for half in (1, 0):
        for db in (1, 2, 3):
            last_go(half, db).wait_recv()
        b = p.z if half else p.x
        total = last_sum[half][b] + last_in[half][0].astype(F32)
        total = total + (last_in[half][1].astype(F32) + last_in[half][2].astype(F32))
        rows = slice(SUM_FEATURES[half][0], sum(SUM_FEATURES[half]))
        own_turned[rows] = inverse * total - own_turned[rows] * slope
    out[...] = jnp.transpose(own_turned[...])

    for x in range(4):
        for zh in range(2):
            swap(x, zh).wait_send()
    for half in halves:
        for way in range(2):
            for kind in range(3):
                near_go(half, way, kind).wait_send()
        for db in (1, 2, 3):
            last_go(half, db).wait_send()
    for copy in [first_dot] + z_dots + x_dots:
        copy.wait_send()

    for piece in range(3):
        for slot in range(9):
            ref = w_of(piece).at[0] if slot < 3 else w_part(piece, 0, 0)
            remote(ref, ref, w_send.at[piece, slot], w_recv.at[piece, 0], p.at(dc=1)).wait_send()
    for half in halves:
        for slot in range(19):
            ref = x_piece(half, 0, 0) if slot < 15 else x_full(half, 0, 0)
            remote(ref, ref, x_send.at[half, slot], x_core.at[half, 0], p.at(dc=1)).wait_send()
    for slot in range(6):
        ref = gains.at[0] if slot < 3 else gain_y
        remote(ref, ref, gain_send.at[slot], gain_recv.at[0], p.at(dc=1)).wait_send()
    for i in range(3):
        remote(g_all.at[0], g_all.at[0], g_send.at[i], g_recv.at[0], p.at(dc=1)).wait_send()
    for dy in (1, 2, 3):
        @pl.when(p.y + dy < 4)
        def _():
            remote(own_kv, own_kv, kv_send.at[dy - 1], kv_recv.at[p.c, p.y], p.at(dc=1)).wait_send()

    for dy in (0, 1, 2, 3):
        @pl.when(p.y >= dy)
        def _():
            remote(own_kv, own_kv, kv_send.at[3 + dy], kv_recv.at[p.c, p.y], p.at(dc=1)).wait_send()

    @pl.loop(0, p.y)
    def _(block):
        core_go(block).wait_send()
        back_go(block).wait_send()

    core_go(p.y).wait_send()


def body(trunk_out, norm_gain, w_query, w_key, value_weight, context_gradient):
    dma, vmem = pltpu.SemaphoreType.DMA, pltpu.VMEM
    halves = []
    for _, rows in SUM_FEATURES:
        halves += [
            vmem((2, 2, rows, 128), BF16),
            vmem((2, 2, rows, 128), BF16),
            vmem((2, 2, 2, rows, 128), BF16),
            vmem((4, rows, 128), F32),
            vmem((4, rows, 128), BF16),
            vmem((3, rows, 128), BF16),
        ]
    return pl.pallas_call(
        backward_kernel,
        out_shape=jax.ShapeDtypeStruct((128, 512), F32),
        in_specs=[ANY, pl.BlockSpec(memory_space=pltpu.VMEM)] + [ANY] * 4,
        out_specs=pl.BlockSpec(memory_space=pltpu.VMEM),
        scratch_shapes=[
            vmem((256, 2048), BF16),
            vmem((256, 256), BF16),
            vmem((256, 256), BF16),
            vmem((128, 2048), BF16),
            vmem((4, 256, 128), BF16),
            vmem((2, 4, 256, 256), BF16),
            vmem((4, 128, Q_COLS), BF16),
            vmem((2, 2, 4, 2, 128, 512), BF16),
            vmem((16, 256, 128), BF16),
            vmem((2, 16, 256, 256), BF16),
            vmem((5, HEAD_SIZE, ROWS), BF16),
            vmem((2, 2, 128, 128), F32),
            vmem((2, 2, 8, 128), F32),
            vmem((512, 128), F32),
            vmem((16, 16, 256), BF16),
            vmem((8, 8, 512), F32),
            vmem((8, ROWS, 512), BF16),
            vmem((4, ROWS, HEAD_SIZE), BF16),
            vmem((4, 128, Q_COLS), BF16),
            vmem((2, 4, ROWS, HEAD_SIZE), BF16),
            vmem((4, HEAD_SIZE, ROWS), BF16),
            vmem((4, HEAD_SIZE, ROWS), BF16),
            vmem((2, HEAD_SIZE, ROWS), BF16),
            vmem((2 * ROWS, HEAD_SIZE), BF16),
            vmem((2, 2, 4, ROWS, ROWS), F32),
            vmem((2, 4, 8, ROWS), F32),
            vmem((2, HEAD_SIZE, ROWS), F32),
            vmem((4, ROWS, HEAD_SIZE), F32),
            vmem((4, ROWS, HEAD_SIZE), F32),
            vmem((2, 4, ROWS, HEAD_SIZE), BF16),
            vmem((4, ROWS, HEAD_SIZE), BF16),
            vmem((4, ROWS, HEAD_SIZE), BF16),
            vmem((4, 2, 2, 512, 128), BF16),
            vmem((5, 2, 2, 8, 128), F32),
            *halves,
            dma((3, 9)), dma((3, 4)), dma((3, 4, 2)),
            dma((2, 19)), dma((2, 4, 4)), dma((2, 4)),
            dma((6,)), dma((4,)), dma((4,)),
            dma((3,)), dma((4,)),
            dma((7,)), dma((2, 4)),
            dma((4,)), dma((4,)), dma((4,)), dma((4,)),
            dma((8,)),
            dma((4, 2)), dma((4, 2)),
            dma((2, 2, 3)), dma((2, 2, 3)),
            dma((2, 3)), dma((2, 3)),
            dma((7,)), dma((7,)),
        ],
        compiler_params=pltpu.CompilerParams(
            collective_id=0, has_side_effects=True, vmem_limit_bytes=60 * 1024 * 1024
        ),
        name="attention_block_backward",
    )(trunk_out, norm_gain, w_query, w_key, value_weight, context_gradient)


def solution(mesh):
    placed = (
        P("ctx", ("grp", "tp")),
        P("grp", "ctx"),
        P("grp", "ctx", "tp"),
        P("grp", "ctx", "tp"),
        P("grp", "ctx", "tp"),
        P("grp", "ctx", "tp"),
    )
    return jax.shard_map(
        body, mesh=mesh, in_specs=placed, out_specs=P("ctx", ("grp", "tp")), check_vma=False
    )
```

```python
import jax
import jax.numpy as jnp
from jax import lax
from jax.experimental import pallas as pl
from jax.experimental.pallas import tpu as pltpu
from jax.sharding import PartitionSpec as P

HEAD_SIZE = 128
EPSILON = 1e-05
MASKED_SCORE = -1e30
LOG2E = 1.4426950408889634
MESH = pl.DeviceIdType.MESH
ANY = pl.BlockSpec(memory_space=pl.ANY)
BF16 = jnp.bfloat16
F32 = jnp.float32
ROWS = 512
OUT_COLS = 4096
Q_COLS = 512
W_COLS = 640


class Place:
    def __init__(self):
        self.x = lax.axis_index("grp")
        ctx = lax.axis_index("ctx")
        self.ctx = ctx
        self.zh = lax.axis_index("tp")
        self.y = lax.div(ctx, 4)
        self.j = lax.rem(ctx, 4)
        self.zl = lax.div(self.j, 2)
        self.c = lax.rem(ctx, 2)
        self.z = self.zh * 2 + self.zl
        self.known = {}
        for dc in range(2):
            self.keep(dc=dc)
            self.keep(dzl=1, dc=dc)
        for d in range(1, 4):
            self.keep(dx=d)
            self.keep(dy=d)
            self.keep(dz=d)

    def keep(self, **deltas):
        deltas = {key: value for key, value in deltas.items() if value}
        self.known[tuple(sorted(deltas.items()))] = self.work_out(**deltas)

    def at(self, **deltas):
        deltas = {key: value for key, value in deltas.items() if not isinstance(value, int) or value}
        key = tuple(sorted(deltas.items()))
        return self.known[key] if key in self.known else self.work_out(**deltas)

    def work_out(self, dx=0, dy=0, dzl=0, dc=0, dz=0):
        def moved(value, step, size):
            return value if isinstance(step, int) and step == 0 else lax.rem(value + step, size)

        x, y, c = moved(self.x, dx, 4), moved(self.y, dy, 4), moved(self.c, dc, 2)
        zl, zh = moved(self.zl, dzl, 2), self.zh
        if dz:
            z = moved(self.z, dz, 4)
            zl, zh = lax.rem(z, 2), lax.div(z, 2)
        return {"grp": x, "ctx": y * 4 + zl * 2 + c, "tp": zh}


def greet(place, partners):
    barrier = pltpu.get_barrier_semaphore()
    for partner in partners:
        pl.semaphore_signal(barrier, inc=1, device_id=place.at(**partner), device_id_type=MESH)
    pl.semaphore_wait(barrier, len(partners))


def remote(src, dst, send_sem, recv_sem, device):
    return pltpu.make_async_remote_copy(
        src_ref=src, dst_ref=dst, send_sem=send_sem, recv_sem=recv_sem, device_id=device, device_id_type=MESH
    )


J_OTHERS = [dict(dc=1), dict(dzl=1), dict(dzl=1, dc=1)]
PARTNERS = J_OTHERS + [{axis: d} for axis in ("dx", "dy", "dz") for d in (1, 2, 3)]
GATHER_ROWS = ((0, 96), (96, 32))
SUM_FEATURES = ((0, 192), (192, 320))


def mm(a, b, contract):
    return lax.dot_general(a, b, ((contract[:1], contract[1:]), ((), ())), preferred_element_type=F32)


def go(src, dst, send_sem, recv_sem, device):
    remote(src, dst, send_sem, recv_sem, device).start()


def arrived(ref, sem):
    pltpu.make_async_copy(ref, ref, sem).wait()


def lanes(index, width=128):
    return pl.ds(pl.multiple_of(index * width, width), width)


def backward_kernel(
    trunk, gain, wq, wk, wv, grads,
    out,
    wq_in, wk_in, wv_in, g_in, kv_cut, q_cut, g_cut,
    x_all, w_kv, w_q, d_turned, inv_ref, inv_rows, own_turned, gains, gain_rows, normed, q_all, g_all, kv, kt, q_turned, g_turned, g_pair, tiles, tops, dq_ref, dk_ref, dv_ref,
    dkv, core_in, back,
    sums, dots,
    relay_in_0, relay_out_0, near_in_0, last_sum_0, last_out_0, last_in_0,
    relay_in_1, relay_out_1, near_in_1, last_sum_1, last_out_1, last_in_1,
    w_send, w_recv, w_set, x_send, x_recv, x_core, gain_send, gain_recv, gain_set, g_send, g_recv,
    kv_send, kv_recv, core_send, core_recv, back_send, back_recv, local,
    swap_send, swap_recv, near_send, near_recv, last_send, last_recv, dot_send, dot_recv,
):
    relay_in, relay_out, near_in = (relay_in_0, relay_in_1), (relay_out_0, relay_out_1), (near_in_0, near_in_1)
    last_sum, last_out, last_in = (last_sum_0, last_sum_1), (last_out_0, last_out_1), (last_in_0, last_in_1)
    p = Place()
    pairs = ((wk.at[0], wk_in), (wv.at[0], wv_in), (wq.at[0], wq_in), (grads.at[0], g_in))
    loads = [pltpu.make_async_copy(src, dst, local.at[i]) for i, (src, dst) in enumerate(pairs)]
    for load in loads:
        load.start()
    greet(p, PARTNERS)

    def j_of(dzl=0, dc=0):
        return lax.rem(p.zl + dzl, 2) * 2 + lax.rem(p.c + dc, 2)

    below, above, across = [lax.rem(p.y + d, 4) for d in (3, 1, 2)]
    j_others = [(j_of(**other), p.at(**other)) for other in J_OTHERS]

    def w_of(piece):
        return w_q.at[piece - 1] if piece else w_kv

    def w_cut(piece):
        return q_cut.at[piece - 1] if piece else kv_cut

    def w_stage(piece):
        cut, ref = w_cut(piece), w_of(piece)
        for j in range(4):
            if piece:
                column = j * Q_COLS + (piece - 1) * 256
                cut[j] = wq_in[:, column : column + 256]
            else:
                cut[j] = (wv_in if j % 2 else wk_in)[:, 128 * (j // 2) : 128 * (j // 2) + 128]
        ref[p.ctx] = cut[p.j]

    def w_leave(piece, partners=(0, 1, 2)):
        cut, ref = w_cut(piece), w_of(piece)
        for i in partners:
            j, device = j_others[i]
            go(cut.at[j], ref.at[p.ctx], w_send.at[piece, i], w_recv.at[piece, p.j], device)

    def w_part(piece, y, part):
        return w_of(piece).at[pl.ds(4 * y + 2 * part, 2)]

    def w_go(piece, y, part, slot, device):
        ref = w_part(piece, y, part)
        go(ref, ref, w_send.at[piece, slot], w_set.at[piece, y, part], device)

    def w_wait(piece, y, part):
        arrived(w_part(piece, y, part), w_set.at[piece, y, part])

    def w_near(piece):
        j, _ = j_others[0]
        arrived(w_of(piece).at[p.y * 4 + j], w_recv.at[piece, j])
        w_go(piece, p.y, p.zl, 3, p.at(dy=1))
        w_go(piece, p.y, p.zl, 4, p.at(dy=3))

    def w_far(piece):
        for j, _ in j_others[1:]:
            arrived(w_of(piece).at[p.y * 4 + j], w_recv.at[piece, j])
        w_go(piece, p.y, 1 - p.zl, 5, p.at(dy=1))
        w_go(piece, p.y, 1 - p.zl, 6, p.at(dy=3))

    def w_relay(piece):
        w_wait(piece, below, 0)
        w_go(piece, below, 0, 7, p.at(dy=1))
        w_wait(piece, above, 1)
        w_go(piece, above, 1, 8, p.at(dy=3))

    def x_a(half, d):
        return lax.rem((p.x if half else p.z) + d, 4)

    def x_b(half, d):
        return lax.rem((p.z if half else p.x) + d, 4)

    def a_device(half, da):
        return p.at(dx=da) if half else p.at(dz=da)

    def b_device(half, db):
        return p.at(dz=db) if half else p.at(dx=db)

    def x_piece(half, x, z):
        return x_all.at[lax.rem(z, 2), p.c, x, lax.div(z, 2), pl.ds(*GATHER_ROWS[half])]

    def x_full(half, b, c):
        if half:
            return x_all.at[lax.rem(b, 2), c, :, lax.div(b, 2), pl.ds(*GATHER_ROWS[1])]
        return x_all.at[:, c, b, :, pl.ds(*GATHER_ROWS[0])]

    def x_at(half, da, db):
        a, b = x_a(half, da), x_b(half, db)
        return (x_piece(1, a, b) if half else x_piece(0, b, a)), x_recv.at[half, a, b]

    def x_go(half, da, db, slot, device, src=None):
        dst, sem = x_at(half, da, db)
        go(dst if src is None else src, dst, x_send.at[half, slot], sem, device)

    def x_first(half):
        own = trunk.at[pl.ds(*GATHER_ROWS[half])]
        for i, d in enumerate((2, 1, 3)):
            x_go(half, 0, 0, i, a_device(half, d), own)
        x_go(half, 0, 0, 3, b_device(half, 1), own)
        x_go(half, 0, 0, 4, b_device(half, 3), own)

    def x_second(half):
        for i, d in enumerate((1, 3, 2)):
            arrived(*x_at(half, d, 0))
            x_go(half, d, 0, 5 + 2 * i, b_device(half, 1))
            x_go(half, d, 0, 6 + 2 * i, b_device(half, 3))

    def x_relay(half):
        for i in range(2):
            arrived(*x_at(half, i, 3))
            x_go(half, i, 3, 11 + 2 * i, b_device(half, 1))
            arrived(*x_at(half, 2 + i, 1))
            x_go(half, 2 + i, 1, 12 + 2 * i, b_device(half, 3))

    def x_to_core(half, d):
        b = x_b(half, d)
        ref = x_full(half, b, p.c)
        go(ref, ref, x_send.at[half, 15 + d], x_core.at[half, b], p.at(dc=1))

    halves = (0, 1)
    for half in halves:
        x_first(half)
    loads[0].wait()
    loads[1].wait()
    w_stage(0)
    w_leave(0)
    own_x = x_all.at[p.zl, p.c, p.x, p.zh]
    pltpu.make_async_copy(trunk, own_x, local.at[5]).start()
    gains[p.ctx] = jnp.broadcast_to(gain[...], (16, 256))
    for i, (j, device) in enumerate(j_others):
        go(gains.at[p.ctx], gains.at[p.ctx], gain_send.at[i], gain_recv.at[p.j], device)
    loads[2].wait()
    w_stage(1)
    w_stage(2)
    w_leave(1, (0,))
    w_near(0)
    w_near(1)
    for half in halves:
        x_second(half)
    w_leave(1, (1, 2))
    w_far(0)
    pltpu.make_async_copy(own_x, own_x, local.at[5]).wait()
    for half in halves:
        x_to_core(half, 0)
    for half in halves:
        x_relay(half)
    for j, _ in j_others:
        arrived(gains.at[p.y * 4 + j], gain_recv.at[j])
    gain_y = gains.at[pl.ds(4 * p.y, 4)]
    for dy in (1, 2, 3):
        go(gain_y, gain_y, gain_send.at[2 + dy], gain_set.at[p.y], p.at(dy=dy))
    w_far(1)
    w_relay(0)
    own_turned[...] = jnp.transpose(own_x[...].astype(F32))
    for half in halves:
        for i in range(2):
            arrived(*x_at(half, 2 + i, 3))
            arrived(*x_at(half, i, 1))
        x_to_core(half, 3)
        x_to_core(half, 1)
    w_leave(2)
    for half in halves:
        for i in range(4):
            arrived(*x_at(half, i, 2))
        x_to_core(half, 2)
    loads[3].wait()
    for j in range(4):
        g_cut[j] = g_in[:, Q_COLS * j : Q_COLS * j + Q_COLS]
    for i, (j, device) in enumerate(j_others):
        go(g_cut.at[j], g_all.at[p.j], g_send.at[i], g_recv.at[p.j], device)
    g_all[p.j] = g_cut[p.j]
    for d in (1, 2, 3):
        y = lax.rem(p.y + d, 4)
        arrived(gains.at[pl.ds(4 * y, 4)], gain_set.at[y])
    for block in range(8):
        row = jnp.concatenate([gains[2 * block][:1], gains[2 * block + 1][:1]], axis=1)
        gain_rows[block] = jnp.broadcast_to(row.astype(F32), (8, 512))
    gain_columns = wq_in

    @pl.loop(0, 8)
    def _(block):
        turned = jnp.transpose(jnp.broadcast_to(gain_rows[block][:1], (128, 512))).astype(BF16)
        gain_columns[:, lanes(2 * block)] = turned[:256]
        gain_columns[:, lanes(2 * block + 1)] = turned[256:]

    w_relay(1)
    w_near(2)
    for half in halves:
        for b in range(4):
            arrived(x_full(half, b, 1 - p.c), x_core.at[half, b])

    def norm_rows(step):
        group = lax.div(step, 4)
        rows = pl.ds(pl.multiple_of(lax.rem(step, 4) * 32, 32), 32)
        zl, c = lax.div(group, 2), lax.rem(group, 2)
        total = jnp.zeros((32, 128), F32)
        for block in range(8):
            part = x_all[zl, c, block // 2, block % 2, rows].astype(F32)
            part = part * part
            total = total + ((part[:, :128] + part[:, 128:256]) + (part[:, 256:384] + part[:, 384:]))
        inverse = lax.rsqrt(jnp.sum(total, axis=1, keepdims=True) * (1.0 / OUT_COLS) + EPSILON)
        inverse = jnp.broadcast_to(inverse, (32, 128))
        inv_ref[zl, c, rows] = inverse
        wide = jnp.concatenate([inverse] * 4, axis=1)
        for block in range(8):
            scaled = x_all[zl, c, block // 2, block % 2, rows].astype(F32) * wide
            scaled = scaled.reshape(4, 8, 512) * gain_rows[block][None]
            row = pl.ds(pl.multiple_of(step * 32, 32), 32)
            normed[block, row] = scaled.reshape(32, 512).astype(BF16)

    def project(piece):
        ref, width = w_of(piece), 256 if piece else 128

        def part(y):
            left = jnp.concatenate([normed[2 * y], normed[2 * y + 1]], axis=1)
            return jnp.dot(left, ref[pl.ds(4 * y, 4)].reshape(1024, width), preferred_element_type=F32)

        total = part(p.y)
        w_wait(piece, below, 1)
        total = total + part(below)
        w_wait(piece, above, 0)
        total = total + part(above)
        w_wait(piece, across, 0)
        w_wait(piece, across, 1)
        return (total + part(across)).astype(BF16)

    def project_heads(piece):
        q = project(piece)
        for i in range(2):
            q_all[2 * piece - 2 + i] = q[:, 128 * i : 128 * i + 128]
            q_turned[2 * piece - 2 + i] = jnp.transpose(q[:, 128 * i : 128 * i + 128])

    @pl.loop(0, 16)
    def _(step):
        norm_rows(step)

    kv[p.c, p.y] = project(0)
    own_kv = kv.at[p.c, p.y]
    for dy in (1, 2, 3):
        @pl.when(p.y + dy < 4)
        def _():
            go(own_kv, own_kv, kv_send.at[dy - 1], kv_recv.at[p.c, p.y], p.at(dy=dy))

    go(own_kv, own_kv, kv_send.at[3], kv_recv.at[p.c, p.y], p.at(dc=1))
    w_far(2)
    for zl in range(2):
        for c in range(2):
            inv_rows[zl, c] = jnp.transpose(inv_ref[zl, c])[:8]
    project_heads(1)
    for dy in (1, 3, 2):
        @pl.when(p.y >= dy)
        def _():
            ref = kv.at[p.c, p.y - dy]
            arrived(ref, kv_recv.at[p.c, p.y - dy])
            go(ref, ref, kv_send.at[3 + dy], kv_recv.at[p.c, p.y - dy], p.at(dc=1))

    for j, _ in j_others:
        arrived(g_all.at[j], g_recv.at[j])
    for dy in (0, 1, 3, 2):
        @pl.when(p.y >= dy)
        def _():
            arrived(kv.at[1 - p.c, p.y - dy], kv_recv.at[1 - p.c, p.y - dy])

    scale = HEAD_SIZE ** -0.5
    factor = scale * LOG2E
    dk_ref[...] = jnp.zeros_like(dk_ref)
    dv_ref[...] = jnp.zeros_like(dv_ref)

    @pl.loop(0, p.y + 1)
    def _(block):
        kt[block] = jnp.transpose(kv[0, block])

    def fold(value, combine):
        parts = [value[8 * i : 8 * i + 8] for i in range(4)]
        return combine(combine(parts[0], parts[1]), combine(parts[2], parts[3]))

    def over(row, count):
        return jnp.broadcast_to(row, (count, ROWS))

    def statistics(head, block, s, t, state, diagonal):
        top, total, delta = state
        tiles[head, 1, block] = t
        parts = [s[32 * i : 32 * i + 32] for i in range(16)]
        if diagonal:
            key = lax.broadcasted_iota(jnp.int32, (32, ROWS), 0)
            row = lax.broadcasted_iota(jnp.int32, (32, ROWS), 1)
            parts = [jnp.where(key <= row - 32 * i, part, MASKED_SCORE) for i, part in enumerate(parts)]
        most = fold(parts[0], jnp.maximum)
        for part in parts[1:]:
            most = jnp.maximum(most, fold(part, jnp.maximum))
        now = jnp.maximum(top, jnp.max(most, axis=0, keepdims=True))
        tops[head, block] = over(now, 8)
        wide = over(now, 32)
        sums = jnp.zeros((8, ROWS), F32)
        deltas = jnp.zeros((8, ROWS), F32)
        for i, part in enumerate(parts):
            e = jnp.exp2((part - wide) * factor)
            tiles[head, 0, block, 32 * i : 32 * i + 32] = e
            sums = sums + fold(e, jnp.add)
            deltas = deltas + fold(e * t[32 * i : 32 * i + 32], jnp.add)
        shrink = jnp.exp2((top - now) * factor)
        total = total * shrink + jnp.sum(sums, axis=0, keepdims=True)
        delta = delta * shrink + jnp.sum(deltas, axis=0, keepdims=True)
        return now, total, delta

    def scores(pair, block, states, diagonal):
        products = []
        for head in range(2):
            s = mm(kv[0, block], q_turned[2 * pair + head], (1, 0))
            products.append((s, mm(kv[1, block], g_turned[head], (1, 0))))
        return tuple(statistics(i, block, *products[i], states[i], diagonal) for i in range(2))

    def lows(head, block, stats):
        top, inverse, delta = stats
        weight = over(jnp.exp2((tops[head, block][:1] - top) * factor) * inverse, 32)
        wide = over(delta, 32)
        probs_low, ds_low = [], []
        for i in range(16):
            chunk = pl.ds(32 * i, 32)
            probs = tiles[head, 0, block, chunk] * weight
            probs_low.append(probs.astype(BF16))
            ds_low.append((probs * (tiles[head, 1, block, chunk] - wide)).astype(BF16))
        return jnp.concatenate(probs_low, axis=0), jnp.concatenate(ds_low, axis=0)

    def pair_grads(pair, block, stats):
        both = [lows(head, block, stats[head]) for head in range(2)]
        for head in range(2):
            dq_ref[head] += mm(kt[block], both[head][1], (1, 0))
        probs = jnp.concatenate([both[0][0], both[1][0]], axis=1)
        ds = jnp.concatenate([both[0][1], both[1][1]], axis=1)
        dv_ref[block] += mm(probs, g_pair[...], (1, 0))
        dk_ref[block] += mm(ds, q_all[pl.ds(2 * pair, 2)].reshape(2 * ROWS, HEAD_SIZE), (1, 0))

    def core_go(block):
        return remote(dkv.at[1 - p.c, block], core_in.at[block], core_send.at[block], core_recv.at[block], p.at(dc=1))

    def back_go(block):
        device = {"grp": p.x, "ctx": block * 4 + p.j, "tp": p.zh}
        return remote(dkv.at[p.c, block], back.at[p.y], back_send.at[block], back_recv.at[p.y], device)

    def to_core(block):
        dkv[0, block] = (dk_ref[block] * scale).astype(BF16)
        dkv[1, block] = dv_ref[block].astype(BF16)
        core_go(block).start()

    def to_rows(block):
        core_go(block).wait_recv()
        dkv[p.c, block] = (dkv[p.c, block].astype(F32) + core_in[block].astype(F32)).astype(BF16)
        back_go(block).start()

    @pl.loop(0, 2)
    def _(pair):
        @pl.when(pair == 1)
        def _():
            project_heads(2)

        for head in range(2):
            g = g_all[:, :, lanes(2 * pair + head)].reshape(ROWS, HEAD_SIZE)
            g_pair[ROWS * head : ROWS * head + ROWS] = g
            g_turned[head] = jnp.transpose(g)
        dq_ref[...] = jnp.zeros_like(dq_ref)
        start = (jnp.full((1, ROWS), MASKED_SCORE, F32), jnp.zeros((1, ROWS), F32), jnp.zeros((1, ROWS), F32))
        states = lax.fori_loop(0, p.y, lambda block, now: scores(pair, block, now, False), (start, start))
        states = scores(pair, p.y, states, True)

        @pl.when(pair == 0)
        def _():
            w_relay(2)

        stats = []
        for top, total, delta in states:
            inverse = 1.0 / total
            stats.append((top, inverse, delta * inverse))

        @pl.loop(0, p.y + 1)
        def _(block):
            pair_grads(pair, block, stats)

            @pl.when(pair == 1)
            def _():
                to_core(block)

                @pl.when(block > 0)
                def _():
                    to_rows(block - 1)

        for head in range(2):
            d_turned[2 * pair + head + 1] = (dq_ref[head] * scale).astype(BF16)

    core_go(p.y).wait_recv()
    dk_ref[0] = dkv[p.c, p.y].astype(F32) + core_in[p.y].astype(F32)
    for dy in (1, 2, 3):
        @pl.when(p.y + dy < 4)
        def _():
            arrived(back.at[p.y + dy], back_recv.at[p.y + dy])
            dk_ref[0] += back[p.y + dy].astype(F32)
    d_turned[0] = jnp.transpose(dk_ref[0]).astype(BF16)

    dot = jnp.zeros((8, ROWS), F32)
    own_turned_kv = jnp.transpose(kv[p.c, p.y])
    for i in range(5):
        for k in range(0, 128, 32):
            turned = q_turned[i - 1, k : k + 32] if i else own_turned_kv[k : k + 32]
            dot = dot + fold(d_turned[i, k : k + 32].astype(F32) * turned.astype(F32), jnp.add)
    dot = jnp.sum(dot, axis=0, keepdims=True)
    for zl in range(2):
        for c in range(2):
            group = zl * 2 + c
            dots[0, c, zl] = jnp.broadcast_to(dot[:, 128 * group : 128 * group + 128], (8, 128)) / inv_rows[zl, c]

    def out_block(x, zh):
        block = x * 2 + zh
        left = [w_of(piece)[pl.ds(2 * block, 2)].reshape(512, 256 if piece else 128) for piece in range(3)]
        part = mm(jnp.concatenate(left, axis=1), d_turned[...].reshape(W_COLS, ROWS), (1, 0))
        for i in range(16):
            rows = slice(32 * i, 32 * i + 32)
            gain_column = gain_columns[32 * (i % 8) : 32 * (i % 8) + 32, lanes(2 * block + i // 8)].astype(F32)
            tiles[zh, 0, x, rows] = part[rows] * jnp.concatenate([gain_column] * 4, axis=1)
        for zl in range(2):
            for i in range(8):
                rows = slice(64 * i, 64 * i + 64)
                normed[block, swap_rows(i), swap_lanes(zl, i)] = tiles[zh, 0, x, rows, lanes(zl * 2 + 1 - p.c)].astype(BF16)

    def swap_rows(i, first=0):
        return slice(first + 64 * (i % 4), first + 64 * (i % 4) + 64)

    def swap_lanes(zl, i):
        first = 128 * (2 * zl + i // 4)
        return slice(first, first + 128)

    def swap_out(x, zh):
        return normed.at[2 * x + zh, pl.ds(0, 256)]

    def swap_in(x, zh):
        return normed.at[2 * x + zh, pl.ds(256, 256)]

    def swap(x, zh):
        return remote(swap_out(x, zh), swap_in(x, zh), swap_send.at[x, zh], swap_recv.at[x, zh], p.at(dc=1))

    def out_blocks(x):
        @pl.loop(0, 2)
        def _(zh):
            out_block(x, zh)
            swap(x, zh).start()

    def add_blocks(x):
        @pl.loop(0, 2)
        def _(zh):
            swap(x, zh).wait_recv()
            for zl in range(2):
                for i in range(8):
                    rows = slice(64 * i, 64 * i + 64)
                    other = normed[2 * x + zh, swap_rows(i, 256), swap_lanes(zl, i)].astype(F32)
                    sums[x, zh, zl, rows] = (tiles[zh, 0, x, rows, lanes(zl * 2 + p.c)] + other).astype(BF16)

    def mine(half, da, part):
        a = x_a(half, da)
        if half:
            return sums.at[a, part, :, pl.ds(*SUM_FEATURES[1])]
        return sums.at[pl.ds(2 * part, 2), lax.div(a, 2), lax.rem(a, 2), pl.ds(*SUM_FEATURES[0])]

    def near_go(half, way, kind):
        step = 3 if way else 1
        if kind == 0:
            src, dst = mine(half, 2, way), relay_in[half].at[way]
        elif kind == 1:
            src, dst = mine(half, step, 1 - way), near_in[half].at[way, 1 - way]
        else:
            src, dst = relay_out[half].at[way], near_in[half].at[way, way]
        return remote(src, dst, near_send.at[half, way, kind], near_recv.at[half, way, kind], a_device(half, step))

    def relay(half, way):
        near_go(half, way, 0).wait_recv()
        step = 3 if way else 1
        total = mine(half, step, way)[...].astype(F32) + relay_in[half][way].astype(F32)
        relay_out[half][way] = total.astype(BF16)
        near_go(half, way, 2).start()

    def last_go(half, db):
        b = x_b(half, db)
        return remote(
            last_out[half].at[b], last_in[half].at[db - 1], last_send.at[half, db - 1], last_recv.at[half, db - 1],
            b_device(half, db),
        )

    def gather_near(half):
        for way in range(2):
            near_go(half, way, 1).wait_recv()
            near_go(half, way, 2).wait_recv()
        for part in range(2):
            total = mine(half, 0, part)[...].astype(F32)
            for way in range(2):
                total = total + near_in[half][way, part].astype(F32)
            last_sum[half][pl.ds(2 * part, 2)] = total
            last_out[half][pl.ds(2 * part, 2)] = total.astype(BF16)
        for db in (2, 1, 3):
            last_go(half, db).start()

    odd = lax.rem(p.x, 2)
    mate = p.x + 1 - 2 * odd
    far, far_mate = lax.rem(p.x + 2, 4), lax.rem(mate + 2, 4)
    far_part = lax.div(far, 2)

    def near_part(part):
        near_go(0, part, 0).start()
        near_go(0, 1 - part, 1).start()

    out_blocks(far)
    out_blocks(far_mate)
    add_blocks(far)
    near_go(1, 0, 0).start()
    near_go(1, 1, 0).start()
    out_blocks(mate)
    add_blocks(far_mate)
    for value in range(2):
        @pl.when(odd == value)
        def _():
            near_go(1, 1 - value, 1).start()

        @pl.when(far_part == value)
        def _():
            near_part(value)

    out_blocks(p.x)
    add_blocks(mate)
    for value in range(2):
        @pl.when(odd == value)
        def _():
            near_go(1, value, 1).start()

    relay(1, 0)
    relay(1, 1)
    add_blocks(p.x)
    for value in range(2):
        @pl.when(far_part == value)
        def _():
            near_part(1 - value)

    def dot_go(slot, src, dst, device):
        return remote(src, dst, dot_send.at[slot], dot_recv.at[slot], device)

    first_dot = dot_go(0, dots.at[0, 1 - p.c], dots.at[1, 0], p.at(dc=1))
    first_dot.start()
    relay(0, 0)
    relay(0, 1)
    first_dot.wait_recv()
    for zl in range(2):
        dots[1, 1, zl] = dots[0, p.c, zl] + dots[1, 0, zl]
    z_dots = [
        dot_go(dz, dots.at[1, 1, lax.rem(p.zl + dz, 2)], dots.at[2, lax.div(dz, 2), dz % 2], p.at(dz=dz))
        for dz in (1, 2, 3)
    ]
    for copy in z_dots:
        copy.start()
    gather_near(1)
    for copy in z_dots:
        copy.wait_recv()
    dots[3, 0, 0] = (dots[1, 1, p.zl] + dots[2, 0, 1]) + (dots[2, 1, 0] + dots[2, 1, 1])
    x_dots = [
        dot_go(3 + dx, dots.at[3, 0, 0], dots.at[4, dx // 2, dx % 2], p.at(dx=dx)) for dx in (1, 2, 3)
    ]
    for copy in x_dots:
        copy.start()
    gather_near(0)
    for copy in x_dots:
        copy.wait_recv()
    dot = (dots[3, 0, 0] + dots[4, 0, 1]) + (dots[4, 1, 0] + dots[4, 1, 1])
    inverse = inv_rows[p.zl, p.c][:1]
    slope = inverse * inverse * inverse * dot[:1] * (1.0 / OUT_COLS)
    for half in (1, 0):
        for db in (1, 2, 3):
            last_go(half, db).wait_recv()
        b = p.z if half else p.x
        total = last_sum[half][b] + last_in[half][0].astype(F32)
        total = total + (last_in[half][1].astype(F32) + last_in[half][2].astype(F32))
        rows = slice(SUM_FEATURES[half][0], sum(SUM_FEATURES[half]))
        own_turned[rows] = inverse * total - own_turned[rows] * slope
    out[...] = jnp.transpose(own_turned[...])

    for x in range(4):
        for zh in range(2):
            swap(x, zh).wait_send()
    for half in halves:
        for way in range(2):
            for kind in range(3):
                near_go(half, way, kind).wait_send()
        for db in (1, 2, 3):
            last_go(half, db).wait_send()
    for copy in [first_dot] + z_dots + x_dots:
        copy.wait_send()

    for piece in range(3):
        for slot in range(9):
            ref = w_of(piece).at[0] if slot < 3 else w_part(piece, 0, 0)
            remote(ref, ref, w_send.at[piece, slot], w_recv.at[piece, 0], p.at(dc=1)).wait_send()
    for half in halves:
        for slot in range(19):
            ref = x_piece(half, 0, 0) if slot < 15 else x_full(half, 0, 0)
            remote(ref, ref, x_send.at[half, slot], x_core.at[half, 0], p.at(dc=1)).wait_send()
    for slot in range(6):
        ref = gains.at[0] if slot < 3 else gain_y
        remote(ref, ref, gain_send.at[slot], gain_recv.at[0], p.at(dc=1)).wait_send()
    for i in range(3):
        remote(g_all.at[0], g_all.at[0], g_send.at[i], g_recv.at[0], p.at(dc=1)).wait_send()
    for dy in (1, 2, 3):
        @pl.when(p.y + dy < 4)
        def _():
            remote(own_kv, own_kv, kv_send.at[dy - 1], kv_recv.at[p.c, p.y], p.at(dc=1)).wait_send()

    for dy in (0, 1, 2, 3):
        @pl.when(p.y >= dy)
        def _():
            remote(own_kv, own_kv, kv_send.at[3 + dy], kv_recv.at[p.c, p.y], p.at(dc=1)).wait_send()

    @pl.loop(0, p.y)
    def _(block):
        core_go(block).wait_send()
        back_go(block).wait_send()

    core_go(p.y).wait_send()


def body(trunk_out, norm_gain, w_query, w_key, value_weight, context_gradient):
    dma, vmem = pltpu.SemaphoreType.DMA, pltpu.VMEM
    halves = []
    for _, rows in SUM_FEATURES:
        halves += [
            vmem((2, 2, rows, 128), BF16),
            vmem((2, 2, rows, 128), BF16),
            vmem((2, 2, 2, rows, 128), BF16),
            vmem((4, rows, 128), F32),
            vmem((4, rows, 128), BF16),
            vmem((3, rows, 128), BF16),
        ]
    return pl.pallas_call(
        backward_kernel,
        out_shape=jax.ShapeDtypeStruct((128, 512), F32),
        in_specs=[ANY, pl.BlockSpec(memory_space=pltpu.VMEM)] + [ANY] * 4,
        out_specs=pl.BlockSpec(memory_space=pltpu.VMEM),
        scratch_shapes=[
            vmem((256, 2048), BF16),
            vmem((256, 256), BF16),
            vmem((256, 256), BF16),
            vmem((128, 2048), BF16),
            vmem((4, 256, 128), BF16),
            vmem((2, 4, 256, 256), BF16),
            vmem((4, 128, Q_COLS), BF16),
            vmem((2, 2, 4, 2, 128, 512), BF16),
            vmem((16, 256, 128), BF16),
            vmem((2, 16, 256, 256), BF16),
            vmem((5, HEAD_SIZE, ROWS), BF16),
            vmem((2, 2, 128, 128), F32),
            vmem((2, 2, 8, 128), F32),
            vmem((512, 128), F32),
            vmem((16, 16, 256), BF16),
            vmem((8, 8, 512), F32),
            vmem((8, ROWS, 512), BF16),
            vmem((4, ROWS, HEAD_SIZE), BF16),
            vmem((4, 128, Q_COLS), BF16),
            vmem((2, 4, ROWS, HEAD_SIZE), BF16),
            vmem((4, HEAD_SIZE, ROWS), BF16),
            vmem((4, HEAD_SIZE, ROWS), BF16),
            vmem((2, HEAD_SIZE, ROWS), BF16),
            vmem((2 * ROWS, HEAD_SIZE), BF16),
            vmem((2, 2, 4, ROWS, ROWS), F32),
            vmem((2, 4, 8, ROWS), F32),
            vmem((2, HEAD_SIZE, ROWS), F32),
            vmem((4, ROWS, HEAD_SIZE), F32),
            vmem((4, ROWS, HEAD_SIZE), F32),
            vmem((2, 4, ROWS, HEAD_SIZE), BF16),
            vmem((4, ROWS, HEAD_SIZE), BF16),
            vmem((4, ROWS, HEAD_SIZE), BF16),
            vmem((4, 2, 2, 512, 128), BF16),
            vmem((5, 2, 2, 8, 128), F32),
            *halves,
            dma((3, 9)), dma((3, 4)), dma((3, 4, 2)),
            dma((2, 19)), dma((2, 4, 4)), dma((2, 4)),
            dma((6,)), dma((4,)), dma((4,)),
            dma((3,)), dma((4,)),
            dma((7,)), dma((2, 4)),
            dma((4,)), dma((4,)), dma((4,)), dma((4,)),
            dma((8,)),
            dma((4, 2)), dma((4, 2)),
            dma((2, 2, 3)), dma((2, 2, 3)),
            dma((2, 3)), dma((2, 3)),
            dma((7,)), dma((7,)),
        ],
        compiler_params=pltpu.CompilerParams(
            collective_id=0, has_side_effects=True, vmem_limit_bytes=60 * 1024 * 1024
        ),
        name="attention_block_backward",
    )(trunk_out, norm_gain, w_query, w_key, value_weight, context_gradient)


def solution(mesh):
    placed = (
        P("ctx", ("grp", "tp")),
        P("grp", "ctx"),
        P("grp", "ctx", "tp"),
        P("grp", "ctx", "tp"),
        P("grp", "ctx", "tp"),
        P("grp", "ctx", "tp"),
    )
    return jax.shard_map(
        body, mesh=mesh, in_specs=placed, out_specs=P("ctx", ("grp", "tp")), check_vma=False
    )
```

```python
import jax
import jax.numpy as jnp
from jax import lax
from jax.experimental import pallas as pl
from jax.experimental.pallas import tpu as pltpu
from jax.sharding import PartitionSpec as P

HEAD_SIZE = 128
EPSILON = 1e-05
MASKED_SCORE = -1e30
LOG2E = 1.4426950408889634
MESH = pl.DeviceIdType.MESH
ANY = pl.BlockSpec(memory_space=pl.ANY)
BF16 = jnp.bfloat16
F32 = jnp.float32
ROWS = 512
OUT_COLS = 4096
Q_COLS = 512
W_COLS = 640


class Place:
    def __init__(self):
        self.x = lax.axis_index("grp")
        ctx = lax.axis_index("ctx")
        self.ctx = ctx
        self.zh = lax.axis_index("tp")
        self.y = lax.div(ctx, 4)
        self.j = lax.rem(ctx, 4)
        self.zl = lax.div(self.j, 2)
        self.c = lax.rem(ctx, 2)
        self.z = self.zh * 2 + self.zl
        self.known = {}
        for dc in range(2):
            self.keep(dc=dc)
            self.keep(dzl=1, dc=dc)
        for d in range(1, 4):
            self.keep(dx=d)
            self.keep(dy=d)
            self.keep(dz=d)

    def keep(self, **deltas):
        deltas = {key: value for key, value in deltas.items() if value}
        self.known[tuple(sorted(deltas.items()))] = self.work_out(**deltas)

    def at(self, **deltas):
        deltas = {key: value for key, value in deltas.items() if not isinstance(value, int) or value}
        key = tuple(sorted(deltas.items()))
        return self.known[key] if key in self.known else self.work_out(**deltas)

    def work_out(self, dx=0, dy=0, dzl=0, dc=0, dz=0):
        def moved(value, step, size):
            return value if isinstance(step, int) and step == 0 else lax.rem(value + step, size)

        x, y, c = moved(self.x, dx, 4), moved(self.y, dy, 4), moved(self.c, dc, 2)
        zl, zh = moved(self.zl, dzl, 2), self.zh
        if dz:
            z = moved(self.z, dz, 4)
            zl, zh = lax.rem(z, 2), lax.div(z, 2)
        return {"grp": x, "ctx": y * 4 + zl * 2 + c, "tp": zh}


def greet(place, partners):
    barrier = pltpu.get_barrier_semaphore()
    for partner in partners:
        pl.semaphore_signal(barrier, inc=1, device_id=place.at(**partner), device_id_type=MESH)
    pl.semaphore_wait(barrier, len(partners))


def remote(src, dst, send_sem, recv_sem, device):
    return pltpu.make_async_remote_copy(
        src_ref=src, dst_ref=dst, send_sem=send_sem, recv_sem=recv_sem, device_id=device, device_id_type=MESH
    )


J_OTHERS = [dict(dc=1), dict(dzl=1), dict(dzl=1, dc=1)]
PARTNERS = J_OTHERS + [{axis: d} for axis in ("dx", "dy", "dz") for d in (1, 2, 3)]
GATHER_ROWS = ((0, 96), (96, 32))
SUM_FEATURES = ((0, 192), (192, 320))


def mm(a, b, contract):
    return lax.dot_general(a, b, ((contract[:1], contract[1:]), ((), ())), preferred_element_type=F32)


def go(src, dst, send_sem, recv_sem, device):
    remote(src, dst, send_sem, recv_sem, device).start()


def arrived(ref, sem):
    pltpu.make_async_copy(ref, ref, sem).wait()


def lanes(index, width=128):
    return pl.ds(pl.multiple_of(index * width, width), width)


def backward_kernel(
    trunk, gain, wq, wk, wv, grads,
    out,
    wq_in, wk_in, wv_in, g_in, kv_cut, q_cut, g_cut,
    x_all, w_kv, w_q, d_turned, inv_ref, inv_rows, own_turned, gains, gain_rows, normed, q_all, g_all, kv, kt, q_turned, g_turned, g_pair, tiles, tops, dq_ref, dk_ref, dv_ref,
    dkv, core_in, back,
    sums, dots,
    relay_in_0, relay_out_0, near_in_0, last_sum_0, last_out_0, last_in_0,
    relay_in_1, relay_out_1, near_in_1, last_sum_1, last_out_1, last_in_1,
    w_send, w_recv, w_set, x_send, x_recv, x_core, gain_send, gain_recv, gain_set, g_send, g_recv,
    kv_send, kv_recv, core_send, core_recv, back_send, back_recv, local,
    swap_send, swap_recv, near_send, near_recv, last_send, last_recv, dot_send, dot_recv,
):
    relay_in, relay_out, near_in = (relay_in_0, relay_in_1), (relay_out_0, relay_out_1), (near_in_0, near_in_1)
    last_sum, last_out, last_in = (last_sum_0, last_sum_1), (last_out_0, last_out_1), (last_in_0, last_in_1)
    p = Place()
    pairs = ((wk.at[0], wk_in), (wv.at[0], wv_in), (wq.at[0], wq_in), (grads.at[0], g_in))
    loads = [pltpu.make_async_copy(src, dst, local.at[i]) for i, (src, dst) in enumerate(pairs)]
    for load in loads:
        load.start()
    greet(p, PARTNERS)

    def j_of(dzl=0, dc=0):
        return lax.rem(p.zl + dzl, 2) * 2 + lax.rem(p.c + dc, 2)

    below, above, across = [lax.rem(p.y + d, 4) for d in (3, 1, 2)]
    j_others = [(j_of(**other), p.at(**other)) for other in J_OTHERS]

    def w_of(piece):
        return w_q.at[piece - 1] if piece else w_kv

    def w_cut(piece):
        return q_cut.at[piece - 1] if piece else kv_cut

    def w_stage(piece):
        cut, ref = w_cut(piece), w_of(piece)
        for j in range(4):
            if piece:
                column = j * Q_COLS + (piece - 1) * 256
                cut[j] = wq_in[:, column : column + 256]
            else:
                cut[j] = (wv_in if j % 2 else wk_in)[:, 128 * (j // 2) : 128 * (j // 2) + 128]
        ref[p.ctx] = cut[p.j]

    def w_leave(piece, partners=(0, 1, 2)):
        cut, ref = w_cut(piece), w_of(piece)
        for i in partners:
            j, device = j_others[i]
            go(cut.at[j], ref.at[p.ctx], w_send.at[piece, i], w_recv.at[piece, p.j], device)

    def w_part(piece, y, part):
        return w_of(piece).at[pl.ds(4 * y + 2 * part, 2)]

    def w_go(piece, y, part, slot, device):
        ref = w_part(piece, y, part)
        go(ref, ref, w_send.at[piece, slot], w_set.at[piece, y, part], device)

    def w_wait(piece, y, part):
        arrived(w_part(piece, y, part), w_set.at[piece, y, part])

    def w_near(piece):
        j, _ = j_others[0]
        arrived(w_of(piece).at[p.y * 4 + j], w_recv.at[piece, j])
        w_go(piece, p.y, p.zl, 3, p.at(dy=1))
        w_go(piece, p.y, p.zl, 4, p.at(dy=3))

    def w_far(piece):
        for j, _ in j_others[1:]:
            arrived(w_of(piece).at[p.y * 4 + j], w_recv.at[piece, j])
        w_go(piece, p.y, 1 - p.zl, 5, p.at(dy=1))
        w_go(piece, p.y, 1 - p.zl, 6, p.at(dy=3))

    def w_relay(piece):
        w_wait(piece, below, 0)
        w_go(piece, below, 0, 7, p.at(dy=1))
        w_wait(piece, above, 1)
        w_go(piece, above, 1, 8, p.at(dy=3))

    def x_a(half, d):
        return lax.rem((p.x if half else p.z) + d, 4)

    def x_b(half, d):
        return lax.rem((p.z if half else p.x) + d, 4)

    def a_device(half, da):
        return p.at(dx=da) if half else p.at(dz=da)

    def b_device(half, db):
        return p.at(dz=db) if half else p.at(dx=db)

    def x_piece(half, x, z):
        return x_all.at[lax.rem(z, 2), p.c, x, lax.div(z, 2), pl.ds(*GATHER_ROWS[half])]

    def x_full(half, b, c):
        if half:
            return x_all.at[lax.rem(b, 2), c, :, lax.div(b, 2), pl.ds(*GATHER_ROWS[1])]
        return x_all.at[:, c, b, :, pl.ds(*GATHER_ROWS[0])]

    def x_at(half, da, db):
        a, b = x_a(half, da), x_b(half, db)
        return (x_piece(1, a, b) if half else x_piece(0, b, a)), x_recv.at[half, a, b]

    def x_go(half, da, db, slot, device, src=None):
        dst, sem = x_at(half, da, db)
        go(dst if src is None else src, dst, x_send.at[half, slot], sem, device)

    def x_first(half):
        own = trunk.at[pl.ds(*GATHER_ROWS[half])]
        for i, d in enumerate((2, 1, 3)):
            x_go(half, 0, 0, i, a_device(half, d), own)
        x_go(half, 0, 0, 3, b_device(half, 1), own)
        x_go(half, 0, 0, 4, b_device(half, 3), own)

    def x_second(half):
        for i, d in enumerate((1, 3, 2)):
            arrived(*x_at(half, d, 0))
            x_go(half, d, 0, 5 + 2 * i, b_device(half, 1))
            x_go(half, d, 0, 6 + 2 * i, b_device(half, 3))

    def x_relay(half):
        for i in range(2):
            arrived(*x_at(half, i, 3))
            x_go(half, i, 3, 11 + 2 * i, b_device(half, 1))
            arrived(*x_at(half, 2 + i, 1))
            x_go(half, 2 + i, 1, 12 + 2 * i, b_device(half, 3))

    def x_to_core(half, d):
        b = x_b(half, d)
        ref = x_full(half, b, p.c)
        go(ref, ref, x_send.at[half, 15 + d], x_core.at[half, b], p.at(dc=1))

    halves = (0, 1)
    for half in halves:
        x_first(half)
    loads[0].wait()
    loads[1].wait()
    w_stage(0)
    w_leave(0)
    own_x = x_all.at[p.zl, p.c, p.x, p.zh]
    pltpu.make_async_copy(trunk, own_x, local.at[5]).start()
    gains[p.ctx] = jnp.broadcast_to(gain[...], (16, 256))
    for i, (j, device) in enumerate(j_others):
        go(gains.at[p.ctx], gains.at[p.ctx], gain_send.at[i], gain_recv.at[p.j], device)
    loads[2].wait()
    w_stage(1)
    w_stage(2)
    w_leave(1)
    w_near(0)
    w_near(1)
    for half in halves:
        x_second(half)
    w_far(0)
    pltpu.make_async_copy(own_x, own_x, local.at[5]).wait()
    for half in halves:
        x_to_core(half, 0)
    for half in halves:
        x_relay(half)
    for j, _ in j_others:
        arrived(gains.at[p.y * 4 + j], gain_recv.at[j])
    gain_y = gains.at[pl.ds(4 * p.y, 4)]
    for dy in (1, 2, 3):
        go(gain_y, gain_y, gain_send.at[2 + dy], gain_set.at[p.y], p.at(dy=dy))
    w_far(1)
    w_relay(0)
    own_turned[...] = jnp.transpose(own_x[...].astype(F32))
    for half in halves:
        for i in range(2):
            arrived(*x_at(half, 2 + i, 3))
            arrived(*x_at(half, i, 1))
        x_to_core(half, 3)
        x_to_core(half, 1)
    w_leave(2)
    for half in halves:
        for i in range(4):
            arrived(*x_at(half, i, 2))
        x_to_core(half, 2)
    loads[3].wait()
    for j in range(4):
        g_cut[j] = g_in[:, Q_COLS * j : Q_COLS * j + Q_COLS]
    for i, (j, device) in enumerate(j_others):
        go(g_cut.at[j], g_all.at[p.j], g_send.at[i], g_recv.at[p.j], device)
    g_all[p.j] = g_cut[p.j]
    w_near(2)
    for d in (1, 2, 3):
        y = lax.rem(p.y + d, 4)
        arrived(gains.at[pl.ds(4 * y, 4)], gain_set.at[y])
    for block in range(8):
        row = jnp.concatenate([gains[2 * block][:1], gains[2 * block + 1][:1]], axis=1)
        gain_rows[block] = jnp.broadcast_to(row.astype(F32), (8, 512))
    gain_columns = wq_in

    @pl.loop(0, 8)
    def _(block):
        turned = jnp.transpose(jnp.broadcast_to(gain_rows[block][:1], (128, 512))).astype(BF16)
        gain_columns[:, lanes(2 * block)] = turned[:256]
        gain_columns[:, lanes(2 * block + 1)] = turned[256:]

    for half in halves:
        for b in range(4):
            arrived(x_full(half, b, 1 - p.c), x_core.at[half, b])

    def norm_rows(step):
        group = lax.div(step, 4)
        rows = pl.ds(pl.multiple_of(lax.rem(step, 4) * 32, 32), 32)
        zl, c = lax.div(group, 2), lax.rem(group, 2)
        total = jnp.zeros((32, 128), F32)
        for block in range(8):
            part = x_all[zl, c, block // 2, block % 2, rows].astype(F32)
            part = part * part
            total = total + ((part[:, :128] + part[:, 128:256]) + (part[:, 256:384] + part[:, 384:]))
        inverse = lax.rsqrt(jnp.sum(total, axis=1, keepdims=True) * (1.0 / OUT_COLS) + EPSILON)
        inverse = jnp.broadcast_to(inverse, (32, 128))
        inv_ref[zl, c, rows] = inverse
        wide = jnp.concatenate([inverse] * 4, axis=1)
        for block in range(8):
            scaled = x_all[zl, c, block // 2, block % 2, rows].astype(F32) * wide
            scaled = scaled.reshape(4, 8, 512) * gain_rows[block][None]
            row = pl.ds(pl.multiple_of(step * 32, 32), 32)
            normed[block, row] = scaled.reshape(32, 512).astype(BF16)

    def project(piece):
        ref, width = w_of(piece), 256 if piece else 128

        def part(y):
            left = jnp.concatenate([normed[2 * y], normed[2 * y + 1]], axis=1)
            return jnp.dot(left, ref[pl.ds(4 * y, 4)].reshape(1024, width), preferred_element_type=F32)

        total = part(p.y)
        w_wait(piece, below, 1)
        total = total + part(below)
        w_wait(piece, above, 0)
        total = total + part(above)
        w_wait(piece, across, 0)
        w_wait(piece, across, 1)
        return (total + part(across)).astype(BF16)

    def project_heads(piece):
        q = project(piece)
        for i in range(2):
            q_all[2 * piece - 2 + i] = q[:, 128 * i : 128 * i + 128]
            q_turned[2 * piece - 2 + i] = jnp.transpose(q[:, 128 * i : 128 * i + 128])

    @pl.loop(0, 8)
    def _(step):
        norm_rows(step)

    w_relay(1)

    @pl.loop(8, 16)
    def _(step):
        norm_rows(step)

    kv[p.c, p.y] = project(0)
    own_kv = kv.at[p.c, p.y]
    for dy in (1, 2, 3):
        @pl.when(p.y + dy < 4)
        def _():
            go(own_kv, own_kv, kv_send.at[dy - 1], kv_recv.at[p.c, p.y], p.at(dy=dy))

    go(own_kv, own_kv, kv_send.at[3], kv_recv.at[p.c, p.y], p.at(dc=1))
    w_far(2)
    for zl in range(2):
        for c in range(2):
            inv_rows[zl, c] = jnp.transpose(inv_ref[zl, c])[:8]
    project_heads(1)
    for dy in (1, 3, 2):
        @pl.when(p.y >= dy)
        def _():
            ref = kv.at[p.c, p.y - dy]
            arrived(ref, kv_recv.at[p.c, p.y - dy])
            go(ref, ref, kv_send.at[3 + dy], kv_recv.at[p.c, p.y - dy], p.at(dc=1))

    for j, _ in j_others:
        arrived(g_all.at[j], g_recv.at[j])
    for dy in (0, 1, 3, 2):
        @pl.when(p.y >= dy)
        def _():
            arrived(kv.at[1 - p.c, p.y - dy], kv_recv.at[1 - p.c, p.y - dy])

    scale = HEAD_SIZE ** -0.5
    factor = scale * LOG2E
    dk_ref[...] = jnp.zeros_like(dk_ref)
    dv_ref[...] = jnp.zeros_like(dv_ref)

    @pl.loop(0, p.y + 1)
    def _(block):
        kt[block] = jnp.transpose(kv[0, block])

    def fold(value, combine):
        parts = [value[8 * i : 8 * i + 8] for i in range(4)]
        return combine(combine(parts[0], parts[1]), combine(parts[2], parts[3]))

    def over(row, count):
        return jnp.broadcast_to(row, (count, ROWS))

    def statistics(head, block, s, t, state, diagonal):
        top, total, delta = state
        tiles[head, 1, block] = t
        parts = [s[32 * i : 32 * i + 32] for i in range(16)]
        if diagonal:
            key = lax.broadcasted_iota(jnp.int32, (32, ROWS), 0)
            row = lax.broadcasted_iota(jnp.int32, (32, ROWS), 1)
            parts = [jnp.where(key <= row - 32 * i, part, MASKED_SCORE) for i, part in enumerate(parts)]
        most = fold(parts[0], jnp.maximum)
        for part in parts[1:]:
            most = jnp.maximum(most, fold(part, jnp.maximum))
        now = jnp.maximum(top, jnp.max(most, axis=0, keepdims=True))
        tops[head, block] = over(now, 8)
        wide = over(now, 32)
        sums = jnp.zeros((8, ROWS), F32)
        deltas = jnp.zeros((8, ROWS), F32)
        for i, part in enumerate(parts):
            e = jnp.exp2((part - wide) * factor)
            tiles[head, 0, block, 32 * i : 32 * i + 32] = e
            sums = sums + fold(e, jnp.add)
            deltas = deltas + fold(e * t[32 * i : 32 * i + 32], jnp.add)
        shrink = jnp.exp2((top - now) * factor)
        total = total * shrink + jnp.sum(sums, axis=0, keepdims=True)
        delta = delta * shrink + jnp.sum(deltas, axis=0, keepdims=True)
        return now, total, delta

    def scores(pair, block, states, diagonal):
        products = []
        for head in range(2):
            s = mm(kv[0, block], q_turned[2 * pair + head], (1, 0))
            products.append((s, mm(kv[1, block], g_turned[head], (1, 0))))
        return tuple(statistics(i, block, *products[i], states[i], diagonal) for i in range(2))

    def lows(head, block, stats):
        top, inverse, delta = stats
        weight = over(jnp.exp2((tops[head, block][:1] - top) * factor) * inverse, 32)
        wide = over(delta, 32)
        probs_low, ds_low = [], []
        for i in range(16):
            chunk = pl.ds(32 * i, 32)
            probs = tiles[head, 0, block, chunk] * weight
            probs_low.append(probs.astype(BF16))
            ds_low.append((probs * (tiles[head, 1, block, chunk] - wide)).astype(BF16))
        return jnp.concatenate(probs_low, axis=0), jnp.concatenate(ds_low, axis=0)

    def pair_grads(pair, block, stats):
        both = [lows(head, block, stats[head]) for head in range(2)]
        for head in range(2):
            dq_ref[head] += mm(kt[block], both[head][1], (1, 0))
        probs = jnp.concatenate([both[0][0], both[1][0]], axis=1)
        ds = jnp.concatenate([both[0][1], both[1][1]], axis=1)
        dv_ref[block] += mm(probs, g_pair[...], (1, 0))
        dk_ref[block] += mm(ds, q_all[pl.ds(2 * pair, 2)].reshape(2 * ROWS, HEAD_SIZE), (1, 0))

    def core_go(block):
        return remote(dkv.at[1 - p.c, block], core_in.at[block], core_send.at[block], core_recv.at[block], p.at(dc=1))

    def back_go(block):
        device = {"grp": p.x, "ctx": block * 4 + p.j, "tp": p.zh}
        return remote(dkv.at[p.c, block], back.at[p.y], back_send.at[block], back_recv.at[p.y], device)

    def to_core(block):
        dkv[0, block] = (dk_ref[block] * scale).astype(BF16)
        dkv[1, block] = dv_ref[block].astype(BF16)
        core_go(block).start()

    def to_rows(block):
        core_go(block).wait_recv()
        dkv[p.c, block] = (dkv[p.c, block].astype(F32) + core_in[block].astype(F32)).astype(BF16)
        back_go(block).start()

    @pl.loop(0, 2)
    def _(pair):
        @pl.when(pair == 1)
        def _():
            project_heads(2)

        for head in range(2):
            g = g_all[:, :, lanes(2 * pair + head)].reshape(ROWS, HEAD_SIZE)
            g_pair[ROWS * head : ROWS * head + ROWS] = g
            g_turned[head] = jnp.transpose(g)
        dq_ref[...] = jnp.zeros_like(dq_ref)
        start = (jnp.full((1, ROWS), MASKED_SCORE, F32), jnp.zeros((1, ROWS), F32), jnp.zeros((1, ROWS), F32))
        states = lax.fori_loop(0, p.y, lambda block, now: scores(pair, block, now, False), (start, start))
        states = scores(pair, p.y, states, True)

        @pl.when(pair == 0)
        def _():
            w_relay(2)

        stats = []
        for top, total, delta in states:
            inverse = 1.0 / total
            stats.append((top, inverse, delta * inverse))

        @pl.loop(0, p.y + 1)
        def _(block):
            pair_grads(pair, block, stats)

            @pl.when(pair == 1)
            def _():
                to_core(block)

                @pl.when(block > 0)
                def _():
                    to_rows(block - 1)

        for head in range(2):
            d_turned[2 * pair + head + 1] = (dq_ref[head] * scale).astype(BF16)

    core_go(p.y).wait_recv()
    dk_ref[0] = dkv[p.c, p.y].astype(F32) + core_in[p.y].astype(F32)
    for dy in (1, 2, 3):
        @pl.when(p.y + dy < 4)
        def _():
            arrived(back.at[p.y + dy], back_recv.at[p.y + dy])
            dk_ref[0] += back[p.y + dy].astype(F32)
    d_turned[0] = jnp.transpose(dk_ref[0]).astype(BF16)

    dot = jnp.zeros((8, ROWS), F32)
    own_turned_kv = jnp.transpose(kv[p.c, p.y])
    for i in range(5):
        for k in range(0, 128, 32):
            turned = q_turned[i - 1, k : k + 32] if i else own_turned_kv[k : k + 32]
            dot = dot + fold(d_turned[i, k : k + 32].astype(F32) * turned.astype(F32), jnp.add)
    dot = jnp.sum(dot, axis=0, keepdims=True)
    for zl in range(2):
        for c in range(2):
            group = zl * 2 + c
            dots[0, c, zl] = jnp.broadcast_to(dot[:, 128 * group : 128 * group + 128], (8, 128)) / inv_rows[zl, c]

    def out_block(x, zh):
        block = x * 2 + zh
        left = [w_of(piece)[pl.ds(2 * block, 2)].reshape(512, 256 if piece else 128) for piece in range(3)]
        part = mm(jnp.concatenate(left, axis=1), d_turned[...].reshape(W_COLS, ROWS), (1, 0))
        for i in range(16):
            rows = slice(32 * i, 32 * i + 32)
            gain_column = gain_columns[32 * (i % 8) : 32 * (i % 8) + 32, lanes(2 * block + i // 8)].astype(F32)
            tiles[zh, 0, x, rows] = part[rows] * jnp.concatenate([gain_column] * 4, axis=1)
        for zl in range(2):
            for i in range(8):
                rows = slice(64 * i, 64 * i + 64)
                normed[block, swap_rows(i), swap_lanes(zl, i)] = tiles[zh, 0, x, rows, lanes(zl * 2 + 1 - p.c)].astype(BF16)

    def swap_rows(i, first=0):
        return slice(first + 64 * (i % 4), first + 64 * (i % 4) + 64)

    def swap_lanes(zl, i):
        first = 128 * (2 * zl + i // 4)
        return slice(first, first + 128)

    def swap_out(x, zh):
        return normed.at[2 * x + zh, pl.ds(0, 256)]

    def swap_in(x, zh):
        return normed.at[2 * x + zh, pl.ds(256, 256)]

    def swap(x, zh):
        return remote(swap_out(x, zh), swap_in(x, zh), swap_send.at[x, zh], swap_recv.at[x, zh], p.at(dc=1))

    def out_blocks(x):
        @pl.loop(0, 2)
        def _(zh):
            out_block(x, zh)
            swap(x, zh).start()

    def add_blocks(x):
        @pl.loop(0, 2)
        def _(zh):
            swap(x, zh).wait_recv()
            for zl in range(2):
                for i in range(8):
                    rows = slice(64 * i, 64 * i + 64)
                    other = normed[2 * x + zh, swap_rows(i, 256), swap_lanes(zl, i)].astype(F32)
                    sums[x, zh, zl, rows] = (tiles[zh, 0, x, rows, lanes(zl * 2 + p.c)] + other).astype(BF16)

    def mine(half, da, part):
        a = x_a(half, da)
        if half:
            return sums.at[a, part, :, pl.ds(*SUM_FEATURES[1])]
        return sums.at[pl.ds(2 * part, 2), lax.div(a, 2), lax.rem(a, 2), pl.ds(*SUM_FEATURES[0])]

    def near_go(half, way, kind):
        step = 3 if way else 1
        if kind == 0:
            src, dst = mine(half, 2, way), relay_in[half].at[way]
        elif kind == 1:
            src, dst = mine(half, step, 1 - way), near_in[half].at[way, 1 - way]
        else:
            src, dst = relay_out[half].at[way], near_in[half].at[way, way]
        return remote(src, dst, near_send.at[half, way, kind], near_recv.at[half, way, kind], a_device(half, step))

    def relay(half, way):
        near_go(half, way, 0).wait_recv()
        step = 3 if way else 1
        total = mine(half, step, way)[...].astype(F32) + relay_in[half][way].astype(F32)
        relay_out[half][way] = total.astype(BF16)
        near_go(half, way, 2).start()

    def last_go(half, db):
        b = x_b(half, db)
        return remote(
            last_out[half].at[b], last_in[half].at[db - 1], last_send.at[half, db - 1], last_recv.at[half, db - 1],
            b_device(half, db),
        )

    def gather_near(half):
        for way in range(2):
            near_go(half, way, 1).wait_recv()
            near_go(half, way, 2).wait_recv()
        for part in range(2):
            total = mine(half, 0, part)[...].astype(F32)
            for way in range(2):
                total = total + near_in[half][way, part].astype(F32)
            last_sum[half][pl.ds(2 * part, 2)] = total
            last_out[half][pl.ds(2 * part, 2)] = total.astype(BF16)
        for db in (2, 1, 3):
            last_go(half, db).start()

    odd = lax.rem(p.x, 2)
    mate = p.x + 1 - 2 * odd
    far, far_mate = lax.rem(p.x + 2, 4), lax.rem(mate + 2, 4)
    far_part = lax.div(far, 2)

    def near_part(part):
        near_go(0, part, 0).start()
        near_go(0, 1 - part, 1).start()

    out_blocks(far)
    out_blocks(far_mate)
    add_blocks(far)
    near_go(1, 0, 0).start()
    near_go(1, 1, 0).start()
    out_blocks(mate)
    add_blocks(far_mate)
    for value in range(2):
        @pl.when(odd == value)
        def _():
            near_go(1, 1 - value, 1).start()

        @pl.when(far_part == value)
        def _():
            near_part(value)

    out_blocks(p.x)
    add_blocks(mate)
    for value in range(2):
        @pl.when(odd == value)
        def _():
            near_go(1, value, 1).start()

    relay(1, 0)
    relay(1, 1)
    add_blocks(p.x)
    for value in range(2):
        @pl.when(far_part == value)
        def _():
            near_part(1 - value)

    def dot_go(slot, src, dst, device):
        return remote(src, dst, dot_send.at[slot], dot_recv.at[slot], device)

    first_dot = dot_go(0, dots.at[0, 1 - p.c], dots.at[1, 0], p.at(dc=1))
    first_dot.start()
    relay(0, 0)
    relay(0, 1)
    first_dot.wait_recv()
    for zl in range(2):
        dots[1, 1, zl] = dots[0, p.c, zl] + dots[1, 0, zl]
    z_dots = [
        dot_go(dz, dots.at[1, 1, lax.rem(p.zl + dz, 2)], dots.at[2, lax.div(dz, 2), dz % 2], p.at(dz=dz))
        for dz in (1, 2, 3)
    ]
    for copy in z_dots:
        copy.start()
    gather_near(1)
    for copy in z_dots:
        copy.wait_recv()
    dots[3, 0, 0] = (dots[1, 1, p.zl] + dots[2, 0, 1]) + (dots[2, 1, 0] + dots[2, 1, 1])
    x_dots = [
        dot_go(3 + dx, dots.at[3, 0, 0], dots.at[4, dx // 2, dx % 2], p.at(dx=dx)) for dx in (1, 2, 3)
    ]
    for copy in x_dots:
        copy.start()
    gather_near(0)
    for copy in x_dots:
        copy.wait_recv()
    dot = (dots[3, 0, 0] + dots[4, 0, 1]) + (dots[4, 1, 0] + dots[4, 1, 1])
    inverse = inv_rows[p.zl, p.c][:1]
    slope = inverse * inverse * inverse * dot[:1] * (1.0 / OUT_COLS)
    for half in (1, 0):
        for db in (1, 2, 3):
            last_go(half, db).wait_recv()
        b = p.z if half else p.x
        total = last_sum[half][b] + last_in[half][0].astype(F32)
        total = total + (last_in[half][1].astype(F32) + last_in[half][2].astype(F32))
        rows = slice(SUM_FEATURES[half][0], sum(SUM_FEATURES[half]))
        own_turned[rows] = inverse * total - own_turned[rows] * slope
    out[...] = jnp.transpose(own_turned[...])

    for x in range(4):
        for zh in range(2):
            swap(x, zh).wait_send()
    for half in halves:
        for way in range(2):
            for kind in range(3):
                near_go(half, way, kind).wait_send()
        for db in (1, 2, 3):
            last_go(half, db).wait_send()
    for copy in [first_dot] + z_dots + x_dots:
        copy.wait_send()

    for piece in range(3):
        for slot in range(9):
            ref = w_of(piece).at[0] if slot < 3 else w_part(piece, 0, 0)
            remote(ref, ref, w_send.at[piece, slot], w_recv.at[piece, 0], p.at(dc=1)).wait_send()
    for half in halves:
        for slot in range(19):
            ref = x_piece(half, 0, 0) if slot < 15 else x_full(half, 0, 0)
            remote(ref, ref, x_send.at[half, slot], x_core.at[half, 0], p.at(dc=1)).wait_send()
    for slot in range(6):
        ref = gains.at[0] if slot < 3 else gain_y
        remote(ref, ref, gain_send.at[slot], gain_recv.at[0], p.at(dc=1)).wait_send()
    for i in range(3):
        remote(g_all.at[0], g_all.at[0], g_send.at[i], g_recv.at[0], p.at(dc=1)).wait_send()
    for dy in (1, 2, 3):
        @pl.when(p.y + dy < 4)
        def _():
            remote(own_kv, own_kv, kv_send.at[dy - 1], kv_recv.at[p.c, p.y], p.at(dc=1)).wait_send()

    for dy in (0, 1, 2, 3):
        @pl.when(p.y >= dy)
        def _():
            remote(own_kv, own_kv, kv_send.at[3 + dy], kv_recv.at[p.c, p.y], p.at(dc=1)).wait_send()

    @pl.loop(0, p.y)
    def _(block):
        core_go(block).wait_send()
        back_go(block).wait_send()

    core_go(p.y).wait_send()


def body(trunk_out, norm_gain, w_query, w_key, value_weight, context_gradient):
    dma, vmem = pltpu.SemaphoreType.DMA, pltpu.VMEM
    halves = []
    for _, rows in SUM_FEATURES:
        halves += [
            vmem((2, 2, rows, 128), BF16),
            vmem((2, 2, rows, 128), BF16),
            vmem((2, 2, 2, rows, 128), BF16),
            vmem((4, rows, 128), F32),
            vmem((4, rows, 128), BF16),
            vmem((3, rows, 128), BF16),
        ]
    return pl.pallas_call(
        backward_kernel,
        out_shape=jax.ShapeDtypeStruct((128, 512), F32),
        in_specs=[ANY, pl.BlockSpec(memory_space=pltpu.VMEM)] + [ANY] * 4,
        out_specs=pl.BlockSpec(memory_space=pltpu.VMEM),
        scratch_shapes=[
            vmem((256, 2048), BF16),
            vmem((256, 256), BF16),
            vmem((256, 256), BF16),
            vmem((128, 2048), BF16),
            vmem((4, 256, 128), BF16),
            vmem((2, 4, 256, 256), BF16),
            vmem((4, 128, Q_COLS), BF16),
            vmem((2, 2, 4, 2, 128, 512), BF16),
            vmem((16, 256, 128), BF16),
            vmem((2, 16, 256, 256), BF16),
            vmem((5, HEAD_SIZE, ROWS), BF16),
            vmem((2, 2, 128, 128), F32),
            vmem((2, 2, 8, 128), F32),
            vmem((512, 128), F32),
            vmem((16, 16, 256), BF16),
            vmem((8, 8, 512), F32),
            vmem((8, ROWS, 512), BF16),
            vmem((4, ROWS, HEAD_SIZE), BF16),
            vmem((4, 128, Q_COLS), BF16),
            vmem((2, 4, ROWS, HEAD_SIZE), BF16),
            vmem((4, HEAD_SIZE, ROWS), BF16),
            vmem((4, HEAD_SIZE, ROWS), BF16),
            vmem((2, HEAD_SIZE, ROWS), BF16),
            vmem((2 * ROWS, HEAD_SIZE), BF16),
            vmem((2, 2, 4, ROWS, ROWS), F32),
            vmem((2, 4, 8, ROWS), F32),
            vmem((2, HEAD_SIZE, ROWS), F32),
            vmem((4, ROWS, HEAD_SIZE), F32),
            vmem((4, ROWS, HEAD_SIZE), F32),
            vmem((2, 4, ROWS, HEAD_SIZE), BF16),
            vmem((4, ROWS, HEAD_SIZE), BF16),
            vmem((4, ROWS, HEAD_SIZE), BF16),
            vmem((4, 2, 2, 512, 128), BF16),
            vmem((5, 2, 2, 8, 128), F32),
            *halves,
            dma((3, 9)), dma((3, 4)), dma((3, 4, 2)),
            dma((2, 19)), dma((2, 4, 4)), dma((2, 4)),
            dma((6,)), dma((4,)), dma((4,)),
            dma((3,)), dma((4,)),
            dma((7,)), dma((2, 4)),
            dma((4,)), dma((4,)), dma((4,)), dma((4,)),
            dma((8,)),
            dma((4, 2)), dma((4, 2)),
            dma((2, 2, 3)), dma((2, 2, 3)),
            dma((2, 3)), dma((2, 3)),
            dma((7,)), dma((7,)),
        ],
        compiler_params=pltpu.CompilerParams(
            collective_id=0, has_side_effects=True, vmem_limit_bytes=60 * 1024 * 1024
        ),
        name="attention_block_backward",
    )(trunk_out, norm_gain, w_query, w_key, value_weight, context_gradient)


def solution(mesh):
    placed = (
        P("ctx", ("grp", "tp")),
        P("grp", "ctx"),
        P("grp", "ctx", "tp"),
        P("grp", "ctx", "tp"),
        P("grp", "ctx", "tp"),
        P("grp", "ctx", "tp"),
    )
    return jax.shard_map(
        body, mesh=mesh, in_specs=placed, out_specs=P("ctx", ("grp", "tp")), check_vma=False
    )
```
